32 devices in a mesh: dom: 32 (over z, y, x, core).
Axes of the slice: x: 2, y: 2, z: 4, core: 2. Of those that a mesh axis runs over, the one named last changes fastest.
Arguments:
- features: bfloat16 [8192, 2048], P('dom'), may hold values from -6 to 6
- weight: bfloat16 [2048, 2048], replicated, may hold values from -0.125 to 0.125
- bias: float32 [2048], replicated, may hold values from -1 to 1
- gamma: float32 [2048], replicated, may hold values from 0.1 to 1.9
- beta: float32 [2048], replicated, may hold values from -3 to 3
- neighbours: int32 [8192, 16], P('dom'), may hold values from 0 to 1279
- edge_mask: int32 [8192, 16], P('dom'), may hold values from 0 to 1, as said below
- node_mask: int32 [8192], P('dom'), may hold values from 0 to 1, as said below
- send_rows: int32 [1024], P('dom'), may hold values from 0 to 255
- send_mask: int32 [1024], P('dom'), may hold values from 0 to 1, as said below
- cotangent: bfloat16 [8192, 2048], P('dom'), may hold values from -6 to 6
Outputs:
- activations: bfloat16 [8192, 2048], P('dom')
- grad_features: bfloat16 [8192, 2048], P('dom')
- grad_weight: float32 [2048, 2048], replicated
- grad_bias: float32 [2048], replicated
- scale_gradient: float32 [2048], replicated
- shift_gradient: float32 [2048], replicated
The draws below stay inside these ranges and needn't reach their ends.
Inputs may be any that keep to these rules, and one draw needn't show every extreme that they name: `edge_mask`: each node's edges fill the first slots of its list; a node has 16, 8, 4, 2 or 1 edges. `node_mask`: the last partition's nodes are all valid. `send_mask`: the live slots of a partition come first; a partition has 32 or 24 live; the first partition has all 32 live.
All inputs are finite; a program needn't handle non-finite values.
Results may differ from the reference program's by a relative error of at most 0.02.
Values may be sent and summed in bfloat16 or wider, within the bound.
No kernel may reach another device: no remote copies, remote signals or barrier semaphores. Data moves between devices by JAX's collectives and lax.ppermute only.
A program may use at most 192 MiB of HBM per device.

```python
import jax
import jax.numpy as jnp
from jax import lax

F = 2048
NODE_DEV = 256
SEND = 32
DEG = 16
NODES = 8192
HALO = 1024
N_DOM = 32


def draw_edge_mask(key, part):
    key = jax.random.fold_in(key, 1)
    level = jax.random.randint(key, (NODES, 1), 0, 5).astype(jnp.int32)
    limit = jnp.right_shift(jnp.int32(DEG), level)
    slots = jnp.arange(DEG, dtype=jnp.int32)[None, :]
    return (slots < limit).astype(jnp.int32)


def draw_node_mask(key, part):
    key = jax.random.fold_in(key, 2)
    places = jnp.arange(N_DOM, dtype=jnp.int32)[:, None]
    lowest = NODE_DEV // 3
    limit = lowest + places * (NODE_DEV - lowest) // max(N_DOM - 1, 1)
    ticket = jax.random.randint(key, (N_DOM, NODE_DEV), 0, NODE_DEV).astype(jnp.int32)
    return (ticket < limit).astype(jnp.int32).reshape(NODES)


def draw_send_mask(key, part):
    key = jax.random.fold_in(key, 3)
    level = jax.random.randint(key, (N_DOM, 1), 0, 2).astype(jnp.int32)
    level = level.at[0, 0].set(0)
    limit = jnp.int32(SEND) - level * jnp.int32(SEND // 4)
    slots = jnp.arange(SEND, dtype=jnp.int32)[None, :]
    return (slots < limit).astype(jnp.int32).reshape(HALO)


def place_ends(drawn, key, smallest, high):
    place = [jax.random.randint(jax.random.fold_in(key, axis), (), 0, length) for axis, length in enumerate(drawn.shape)]
    longest = drawn.shape.index(max(drawn.shape))
    neighbour = place[:longest] + [(place[longest] + 1) % drawn.shape[longest]] + place[longest + 1:]
    return drawn.at[tuple(place)].set(smallest).at[tuple(neighbour)].set(high)


def shard_levels(stream_key, extent, cuts, least, largest):
    level, own = 1.0, jax.random.fold_in(stream_key, 6)
    for axis_at, blocks in cuts:
        draws = jnp.exp(jax.random.uniform(jax.random.fold_in(own, axis_at), (blocks,), jnp.float32, least / len(cuts), largest / len(cuts)))
        level = level * jnp.repeat(draws, extent[axis_at] // blocks).reshape([-1 if axis == axis_at else 1 for axis in range(len(extent))])
    return level


def gaussian(key, extent, spread, reach, split=(), kind=jnp.bfloat16):
    gain = shard_levels(key, extent, split, -0.22, 0.18) if split else 1.0
    result = jax.random.normal(key, extent, jnp.float32) * spread * gain
    return jnp.minimum(jnp.maximum(result, -reach), reach).astype(kind)


def setup_inputs(seed: int = 0) -> dict:
    key_list = jax.random.split(jax.random.key(seed), 12)
    features = gaussian(key_list[0], (NODES, F), 1.0, 6.0, ((0, 32),))
    weight = gaussian(key_list[1], (F, F), F ** -0.5, 0.125)
    bias = jnp.clip(jax.random.uniform(key_list[2], (F,), jnp.float32, -1.0, 1.0), -1.0, 1.0)
    gamma = jnp.clip(1.0 + 0.18 * jax.random.normal(key_list[3], (F,), jnp.float32), 0.1, 1.9)
    beta = gaussian(key_list[4], (F,), 0.5, 3.0, (), jnp.float32)
    neighbours = place_ends(jax.random.randint(key_list[5], (NODES, DEG), 0, NODE_DEV + HALO), jax.random.fold_in(key_list[5], 1), 0, (NODE_DEV + HALO) - 1).astype(jnp.int32)
    edge_mask = draw_edge_mask(jax.random.fold_in(key_list[11], 71), 0)
    node_mask = draw_node_mask(jax.random.fold_in(key_list[11], 71), 0)
    send_rows = place_ends(jax.random.randint(key_list[8], (HALO,), 0, NODE_DEV), jax.random.fold_in(key_list[8], 1), 0, NODE_DEV - 1).astype(jnp.int32)
    send_mask = draw_send_mask(jax.random.fold_in(key_list[11], 71), 0)
    cotangent = gaussian(key_list[10], (NODES, F), 1.0, 6.0, ((0, 32),))
    return dict(features=features, weight=weight, bias=bias, gamma=gamma, beta=beta, neighbours=neighbours, edge_mask=edge_mask, node_mask=node_mask, send_rows=send_rows, send_mask=send_mask, cotangent=cotangent)


@jax.custom_vjp
def low(v):
    return lax.optimization_barrier(v.astype(jnp.bfloat16)).astype(jnp.float32)

@jax.custom_vjp
def low_back(v):
    return v

def low_keep(v):
    return (low(v), None)

def low_pass(kept, grad):
    return (grad,)

def back_keep(v):
    return (v, None)

def back_low(kept, grad):
    return (low(grad),)
low.defvjp(low_keep, low_pass)
low_back.defvjp(back_keep, back_low)

def reference(features, weight, bias, gamma, beta, neighbours, edge_mask, node_mask, send_rows, send_mask, cotangent):
    owner = jnp.arange(HALO, dtype=jnp.int32) // SEND
    send_global = (owner * NODE_DEV + send_rows).astype(jnp.int32)
    part_of = jnp.arange(NODES, dtype=jnp.int32) // NODE_DEV
    index = jnp.where(neighbours < NODE_DEV, part_of[:, None] * NODE_DEV + neighbours, NODES + neighbours - NODE_DEV).astype(jnp.int32)
    emask = edge_mask.astype(jnp.float32)
    inverse = 1.0 / (lax.optimization_barrier(jnp.sum(emask, axis=1)) + 1.0)
    valid_rows_mask = node_mask.astype(jnp.float32)[:, None]
    valid_count = jnp.sum(valid_rows_mask)
    live = send_mask.astype(jnp.float32)[:, None]

    def forward(feats, wmat, bvec, gvec, svec):
        halo = feats[send_global] * live
        table = jnp.concatenate([feats, halo], axis=0)
        total = 2.0 * feats
        for slot in range(DEG):
            total = total + emask[:, slot:slot + 1] * table[index[:, slot]]
        agg = low(total * inverse[:, None])
        zval = low_back(jnp.dot(agg, wmat, precision=lax.Precision.HIGHEST) + bvec)
        yval = jax.nn.silu(zval)
        mean = lax.optimization_barrier(jnp.sum(yval * valid_rows_mask, axis=0)) / valid_count
        centered_values = yval - mean
        var = lax.optimization_barrier(jnp.sum(centered_values * centered_values * valid_rows_mask, axis=0)) / valid_count
        return valid_rows_mask * (gvec * centered_values * lax.rsqrt(var + 1e-05) + svec)
    outputs, pullback = jax.vjp(forward, features.astype(jnp.float32), weight.astype(jnp.float32), bias, gamma, beta)
    grads = pullback(cotangent.astype(jnp.float32))
    return (outputs.astype(jnp.bfloat16), grads[0].astype(jnp.bfloat16), grads[1], grads[2], grads[3], grads[4])
```

```python
import functools

import jax
import jax.numpy as jnp
from jax import lax
from jax.experimental import pallas as pl
from jax.experimental.pallas import tpu as pltpu
from jax.sharding import PartitionSpec as P

BF = jnp.bfloat16
F32 = jnp.float32


def dot(a, b, dims=((1,), (0,))):
    return lax.dot_general(a, b, (dims, ((), ())), preferred_element_type=F32)


def place_kernel(where, piece, total, out):
    out[...] = piece[...].astype(out.dtype)


def place(total, piece, row_xor, column_block, blocks, shape):
    rows, w = piece.shape
    block = rows // blocks
    where = jnp.stack([row_xor, column_block]).astype(jnp.int32)
    operands = [where, piece]
    in_specs = [pl.BlockSpec((block, w), lambda i, s: (i ^ s[0], 0))]
    aliases = {}
    if total is not None:
        operands.append(total)
        in_specs.append(pl.BlockSpec(memory_space=pl.ANY))
        aliases = {2: 0}
        body = place_kernel
    else:
        def body(where, piece, out):
            place_kernel(where, piece, None, out)
    return pl.pallas_call(
        body,
        out_shape=jax.ShapeDtypeStruct(shape, F32),
        grid_spec=pltpu.PrefetchScalarGridSpec(
            num_scalar_prefetch=1,
            grid=(blocks,),
            in_specs=in_specs,
            out_specs=pl.BlockSpec((block, w), lambda i, s: (i, s[1])),
        ),
        input_output_aliases=aliases,
        name="place",
    )(*operands)


def on_device(
    size,
    features,
    weight,
    bias,
    gamma,
    beta,
    neighbours,
    edge_mask,
    node_mask,
    send_rows,
    send_mask,
    cotangent,
):
    nodes, width = features.shape
    slots = neighbours.shape[1]
    sends = send_rows.shape[0]
    half = width // 2
    quarter = width // 4
    rest = list(range(3, size.bit_length() - 1))

    me = lax.axis_index("dom")
    core = me & 1
    is0 = core == 0
    b1, b2 = (me >> 1) & 1, (me >> 2) & 1
    first = jnp.where(is0, b1, b2)
    second = jnp.where(is0, b2, b1)
    first_weight = jnp.where(is0, 2, 4)
    second_weight = 6 - first_weight

    def bit(b):
        return (me >> b) & 1

    core_perm = [(i, i ^ 1) for i in range(size)]
    first_perm = [(i, i ^ (4 if i & 1 else 2)) for i in range(size)]
    second_perm = [(i, i ^ (2 if i & 1 else 4)) for i in range(size)]

    def send(x, perm):
        return lax.ppermute(x, "dom", perm)

    def swap(x):
        return send(x, core_perm)

    def along(x, b):
        return send(x, [(i, i ^ (1 << b)) for i in range(size)])

    def mine(x):
        return lax.dynamic_slice_in_dim(x, core * half, half, x.ndim - 1)

    def other(x):
        return lax.dynamic_slice_in_dim(x, (1 - core) * half, half, x.ndim - 1)

    def ordered(own, sibling, axis):
        return jnp.where(
            is0, jnp.concatenate([own, sibling], axis), jnp.concatenate([sibling, own], axis)
        )

    live_row = jnp.where(send_mask > 0, send_rows, -1)
    rows_hot = (live_row[:, None] == jnp.arange(nodes)[None, :]).astype(BF)
    outgoing = dot(rows_hot, features).astype(BF)
    halo = jnp.concatenate([mine(outgoing), swap(other(outgoing))], 0)
    for b in reversed(rest):
        halo = jnp.concatenate([halo, along(halo, b)], 0)
    halo = jnp.concatenate([halo, send(halo, second_perm)], 0)
    halo = jnp.concatenate([halo, send(halo, first_perm)], 0)

    live_neighbour = jnp.where(edge_mask > 0, neighbours, -1)
    packed = jnp.concatenate([live_neighbour, node_mask[:, None]], 1)
    packed = ordered(packed, swap(packed), 0)
    chip_neighbours, valid = packed[:, :slots], packed[:, slots:].astype(F32)
    inverse = 1.0 / (jnp.sum((chip_neighbours >= 0).astype(F32), 1, keepdims=True) + 1.0)
    chip_features = ordered(mine(features), swap(other(features)), 0)
    grad_in = ordered(mine(cotangent), swap(other(cotangent)), 0)

    halo_rows = sends * size
    place_of = jnp.arange(halo_rows)
    chip, row = place_of // (2 * sends), place_of % (2 * sends)
    levels = len(rest)
    relative = ((chip >> (levels + 1)) & 1) * first_weight + ((chip >> levels) & 1) * second_weight
    for k, b in enumerate(rest):
        relative = relative + (((chip >> (levels - 1 - k)) & 1) << b)
    owner = (me ^ relative) ^ (row // sends)
    label = nodes + owner * sends + row % sends

    def counts(lists, labels):
        total = 0.0
        for e in range(slots):
            total = total + jnp.where(lists[:, e : e + 1] == labels[None, :], 1.0, 0.0)
        return total

    halo_count = counts(chip_neighbours, label).astype(BF)
    local = jnp.arange(nodes)
    own_count = counts(chip_neighbours, local) + jnp.where(
        jnp.arange(2 * nodes)[:, None] % nodes == local[None, :], 2.0, 0.0
    )
    own_count = own_count.astype(BF).reshape(2, nodes, nodes)

    def per_core(a, b, contract):
        return lax.dot_general(
            a, b.reshape(2, nodes, half), (((contract,), (1,)), ((0,), (0,))), preferred_element_type=F32
        ).reshape(2 * nodes, half)

    own_sum = per_core(own_count, chip_features, 2)
    agg_mine = ((dot(halo_count, halo) + own_sum) * inverse).astype(BF)
    agg_other = swap(agg_mine)
    weight_mine = lax.dynamic_slice(weight, (core * half, core * half), (half, half))
    weight_other = lax.dynamic_slice(weight, ((1 - core) * half, core * half), (half, half))
    z = dot(agg_mine, weight_mine) + dot(agg_other, weight_other) + mine(bias)
    sigma = jax.nn.sigmoid(z)
    y = z * sigma
    slope = sigma * (1.0 + z * (1.0 - sigma)) * valid
    g = grad_in.astype(F32) * valid

    count = jnp.sum(valid)
    y_sum = jnp.sum(y * valid, 0)
    centred = (y - y_sum / jnp.maximum(count, 1.0)) * valid
    stats = jnp.stack(
        [
            jnp.full((half,), count),
            y_sum,
            jnp.sum(centred * centred, 0),
            jnp.sum(g, 0),
            jnp.sum(g * centred, 0),
            jnp.sum(slope * g, 0),
            jnp.sum(slope, 0),
            jnp.sum(slope * centred, 0),
        ]
    )

    def merge(own, received, upper):
        a, b = jnp.where(upper, received, own), jnp.where(upper, own, received)
        na, nb = a[0], b[0]
        n = na + nb
        ma, mb = a[1] / jnp.maximum(na, 1.0), b[1] / jnp.maximum(nb, 1.0)
        m = (a[1] + b[1]) / jnp.maximum(n, 1.0)
        da, db = ma - m, mb - m
        return jnp.stack(
            [
                n,
                a[1] + b[1],
                (a[2] + na * da * da) + (b[2] + nb * db * db),
                a[3] + b[3],
                (a[4] + da * a[3]) + (b[4] + db * b[3]),
                a[5] + b[5],
                a[6] + b[6],
                (a[7] + da * a[6]) + (b[7] + db * b[6]),
            ]
        )

    for b in rest:
        stats = merge(stats, along(stats, b), bit(b) == 1)
    stats = merge(stats, send(stats, first_perm), first == 1)
    stats = merge(stats, send(stats, second_perm), second == 1)
    n = stats[0]
    mean = stats[1] / n
    inverse_deviation = lax.rsqrt(stats[2] / n + 1e-05)
    shift_gradient = stats[3]
    scale_gradient = inverse_deviation * stats[4]
    gain = mine(gamma) * inverse_deviation
    bias_gradient = gain * (
        stats[5] - shift_gradient / n * stats[6] - inverse_deviation * scale_gradient / n * stats[7]
    )
    vectors = jnp.stack([bias_gradient, scale_gradient, shift_gradient])
    vectors = ordered(vectors, swap(vectors), 1)

    normalized = (y - mean) * inverse_deviation
    activations = (valid * (mine(gamma) * normalized + mine(beta))).astype(BF)
    dy = gain * (g - shift_gradient / n - normalized * (scale_gradient / n))
    dz_wide = dy * slope
    dz = dz_wide.astype(BF)
    dz_scaled = (dz_wide * inverse).astype(BF)

    def rows_of(x, k):
        return lax.dynamic_slice_in_dim(x, k * nodes, nodes, 0)

    activations = ordered(rows_of(activations, core), swap(rows_of(activations, 1 - core)), 1)

    same = second == core
    agg_keep = jnp.where(same, agg_mine, agg_other)
    agg_send = jnp.where(same, agg_other, agg_mine)
    agg_keep = jnp.concatenate([agg_keep, send(agg_keep, first_perm)], 0)
    agg_send = jnp.concatenate([agg_send, send(agg_send, first_perm)], 0)
    dz_keep = lax.dynamic_slice_in_dim(dz, first * quarter, quarter, 1)
    dz_send = lax.dynamic_slice_in_dim(dz, (1 - first) * quarter, quarter, 1)
    dz_pair = jnp.concatenate([dz_keep, send(dz_send, first_perm)], 0)
    by_rows = ((0,), (0,))
    received = send(dot(agg_send, dz_pair, by_rows).astype(BF), second_perm)
    part = (dot(agg_keep, dz_pair, by_rows) + received.astype(F32)).astype(BF)
    for b in rest:
        rows = part.shape[0] // 2
        out = lax.dynamic_slice_in_dim(part, (1 - bit(b)) * rows, rows, 0)
        keep = lax.dynamic_slice_in_dim(part, bit(b) * rows, rows, 0)
        part = (keep.astype(F32) + along(out, b).astype(F32)).astype(BF)
    for b in reversed(rest):
        part = jnp.concatenate([part, along(part, b)], 0)
    part = jnp.concatenate([part, send(part, second_perm)], 0)
    blocks = size // 4
    low = 0
    for k, b in enumerate(rest):
        low = low + (bit(b) << (levels - 1 - k))
    own_xor, sibling_xor = (second << levels) + low, (first << levels) + low
    pair = send(part, first_perm)
    shape = (width, width)
    total = place(None, part, own_xor, core * 2 + first, blocks, shape)
    total = place(total, swap(part), sibling_xor, (1 - core) * 2 + second, blocks, shape)
    total = place(total, pair, own_xor, core * 2 + 1 - first, blocks, shape)
    total = place(total, swap(pair), sibling_xor, (1 - core) * 2 + 1 - second, blocks, shape)

    cut = halo_rows // 2
    received = send(dot(halo_count[:, cut:], dz_scaled, by_rows).astype(BF), first_perm)
    back = dot(halo_count[:, :cut], dz_scaled, by_rows) + received.astype(F32)
    for hop in [second_perm] + [[(i, i ^ (1 << b)) for i in range(size)] for b in rest]:
        cut = cut // 2
        back = back[:cut] + send(back[cut:].astype(BF), hop).astype(F32)
    back = back.astype(BF)
    own_back = per_core(own_count, dz_scaled, 1)
    back_rows = ordered(back[:sends], swap(back[sends:]), 1)
    own_rows = ordered(
        rows_of(own_back, core).astype(BF), swap(rows_of(own_back, 1 - core).astype(BF)), 1
    )
    table_back = (own_rows.astype(F32) + dot(rows_hot, back_rows, by_rows)).astype(BF)
    grad_features = dot(table_back, weight, ((1,), (1,))).astype(BF)
    return activations, grad_features, total, vectors[0], vectors[1], vectors[2]


def solution(mesh):
    size = mesh.shape["dom"]
    return jax.shard_map(
        functools.partial(on_device, size),
        mesh=mesh,
        in_specs=(
            P("dom", None),
            P(),
            P(),
            P(),
            P(),
            P("dom", None),
            P("dom", None),
            P("dom"),
            P("dom"),
            P("dom"),
            P("dom", None),
        ),
        out_specs=(P("dom", None), P("dom", None), P(), P(), P(), P()),
        check_vma=False,
    )
```

```python
import functools

import jax
import jax.numpy as jnp
from jax import lax
from jax.experimental import pallas as pl
from jax.experimental.pallas import tpu as pltpu
from jax.sharding import PartitionSpec as P

BF = jnp.bfloat16
F32 = jnp.float32
MIB = 1 << 20
HALO_WAYS = ((512, "z1 z0 s f"), (512, "z1 z0 s f"))
BACK_WAY = "s f z0 z1"
TILES = 2

FREE = pl.CostEstimate(flops=0, bytes_accessed=0, transcendentals=0)
SMALL = pl.CostEstimate(flops=0, bytes_accessed=2 * MIB, transcendentals=0)
HBM = pl.BlockSpec(memory_space=pltpu.HBM)
SMEM = pl.BlockSpec(memory_space=pltpu.SMEM)
VMEM = pl.BlockSpec(memory_space=pltpu.VMEM)
BY_ROWS = (((0,), (0,)), ((), ()))


def shape_of(shape, dtype):
    return jax.ShapeDtypeStruct(shape, dtype)


def far_shape(shape, dtype):
    return pltpu.HBM(shape, dtype)


def call(body, out_shape, name, vmem=24, cost=FREE, **rest):
    kernel = pl.pallas_call(
        body,
        out_shape=out_shape,
        compiler_params=pltpu.CompilerParams(vmem_limit_bytes=vmem * MIB),
        cost_estimate=cost,
        name=name,
        **rest,
    )
    specs = rest.get("in_specs")

    def run(*operands):
        if specs is None:
            return kernel(*operands)
        return kernel(
            *[
                pltpu.with_memory_space_constraint(x, pltpu.HBM) if spec is HBM else x
                for x, spec in zip(operands, specs)
            ]
        )

    return run


def scalars(*x):
    return jnp.stack([jnp.int32(v) for v in x])


def mxu(a, b):
    return jnp.dot(a, b, preferred_element_type=F32)


def by_rows(a, b):
    return lax.dot_general(a, b, BY_ROWS, preferred_element_type=F32)


def copy_all(copies):
    for c in copies:
        c.start()
    for c in copies:
        c.wait()


def outgoing_kernel(where, rows, features, away, *keep):
    nodes, width = features.shape
    half = width // 2
    hot = (rows[...] == lax.broadcasted_iota(jnp.int32, (rows.shape[0], nodes), 1)).astype(BF)
    there = features[:, pl.ds(pl.multiple_of((1 - where[0]) * half, half), half)]
    away[...] = mxu(hot, there).astype(BF)
    here = mxu(hot, features[:, pl.ds(pl.multiple_of(where[0] * half, half), half)]).astype(BF)
    at = 0
    for out in keep:
        out[...] = here[:, at : at + out.shape[1]]
        at += out.shape[1]


def outgoing_rows(core, rows, features, widths):
    sends, half = rows.shape[0], features.shape[1] // 2
    return call(
        outgoing_kernel,
        tuple(shape_of((sends, w), BF) for w in (half,) + widths),
        "outgoing",
        in_specs=[SMEM, VMEM, VMEM],
    )(scalars(core), rows, features)


def stack_kernel(n, received, *refs):
    own, outs = refs[:n], refs[n:]
    at = 0
    for x, out in zip(own, outs):
        rows, w = x.shape
        out[:rows, :] = x[...]
        out[rows:, :] = received[:, at : at + w]
        at += w


def stack(own, received):
    return call(
        functools.partial(stack_kernel, len(own)),
        tuple(shape_of((2 * x.shape[0], x.shape[1]), BF) for x in own),
        "stack",
    )(received, *own)


def interleave_kernel(outer, own, received, out):
    step = own.shape[0] // outer
    for a in range(outer):
        out[2 * a * step : (2 * a + 1) * step, :] = own[a * step : (a + 1) * step, :]
        out[(2 * a + 1) * step : (2 * a + 2) * step, :] = received[a * step : (a + 1) * step, :]


def interleave(own, received, outer):
    rows, w = own.shape
    return call(
        functools.partial(interleave_kernel, outer), shape_of((2 * rows, w), own.dtype), "interleave"
    )(own, received)


def counts_kernel(packed, label, halo_count, own_count, factors):
    nodes, columns = packed.shape
    slots = columns - 1

    def count(labels):
        total = jnp.zeros((nodes, labels.shape[1]), F32)
        for e in range(slots):
            total = total + jnp.where(packed[:, e : e + 1] == labels, 1.0, 0.0)
        return total

    halo_count[...] = count(label[...]).astype(BF)
    local = lax.broadcasted_iota(jnp.int32, (nodes, nodes), 1)
    row = lax.broadcasted_iota(jnp.int32, (nodes, nodes), 0)
    own_count[...] = (count(local) + jnp.where(row == local, 2.0, 0.0)).astype(BF)
    degree = jnp.zeros((nodes, 1), F32)
    for e in range(slots):
        degree = degree + jnp.where(packed[:, e : e + 1] >= 0, 1.0, 0.0)
    lane = lax.broadcasted_iota(jnp.int32, factors.shape, 1)
    factors[...] = jnp.where(lane == 0, packed[:, slots:].astype(F32), 1.0 / (degree + 1.0))


def counts(packed, label):
    nodes = packed.shape[0]
    return call(
        counts_kernel,
        (
            shape_of((nodes, label.shape[1]), BF),
            shape_of((nodes, nodes), BF),
            shape_of((nodes, 128), F32),
        ),
        "counts",
    )(packed, label)


def split_kernel(where, features, cotangent, feature_out, cotangent_out, sem):
    half = features.shape[1] // 2
    away = pl.ds(pl.multiple_of((1 - where[0]) * half, half), half)
    copy_all(
        [
            pltpu.make_async_copy(features.at[:, away], feature_out, sem.at[0]),
            pltpu.make_async_copy(cotangent.at[:, away], cotangent_out, sem.at[1]),
        ]
    )


def split(core, features, cotangent):
    rows, width = features.shape
    out = shape_of((rows, width // 2), BF)
    return call(
        split_kernel,
        (out, out),
        "split",
        in_specs=[SMEM, HBM, HBM],
        out_specs=(VMEM, VMEM),
        scratch_shapes=[pltpu.SemaphoreType.DMA((2,))],
    )(scalars(core), features, cotangent)


def aggregate_kernel(n, where, features, feature_in, *refs):
    own, sibling, halos = refs[:3], refs[3:6], refs[6 : 6 + n]
    first, second, near_own, sem = refs[6 + n :]
    nodes, half = near_own.shape
    core = where[0]
    here = pl.ds(pl.multiple_of(core * half, half), half)
    copy = pltpu.make_async_copy(features.at[:, here], near_own, sem)
    copy.start()

    def means(side, table):
        halo_count, own_count, factors = side
        start = 0
        parts = []
        for halo in halos:
            part = slice(start, start + halo.shape[1])
            total = mxu(halo_count[...], halo[...]) + mxu(own_count[...], table[:, part])
            parts.append((part, (total * factors[:, 1:2]).astype(BF)))
            start += halo.shape[1]
        return parts

    for k, (side, table) in enumerate(((sibling, feature_in), (own, near_own))):
        if k == 1:
            copy.wait()
        parts = means(side, table)
        for part, value in parts:
            for flag, out in ((k == 1, first), (k == 0, second)):

                @pl.when((core == 0) == flag)
                def _():
                    out[:, part] = value


def aggregate(core, features, feature_in, own, sibling, halos):
    rows, half = feature_in.shape
    out = shape_of((rows, half), BF)
    return call(
        functools.partial(aggregate_kernel, len(halos)),
        (out, out),
        "aggregate",
        in_specs=[SMEM, HBM] + [VMEM] * (7 + len(halos)),
        scratch_shapes=[pltpu.VMEM((rows, half), BF), pltpu.SemaphoreType.DMA],
    )(scalars(core), features, feature_in, *own, *sibling, *halos)


def grad_loads(core, cotangent, cotangent_in, near_g, column, sems):
    rows, half = cotangent_in.shape
    start, size = column
    whole = pl.ds(pl.multiple_of(core * half + start, 256), size)
    part = pl.ds(pl.multiple_of(start, 256), size)
    own = pl.ds(pl.multiple_of(core * rows, rows), rows)
    far = pl.ds(pl.multiple_of((1 - core) * rows, rows), rows)
    return [
        pltpu.make_async_copy(cotangent.at[:, whole], near_g.at[own, part], sems.at[0]),
        pltpu.make_async_copy(cotangent_in.at[:, part], near_g.at[far, part], sems.at[1]),
    ]


def forward_kernel(
    where, first_mine, second_mine, first_other, second_other, bias, own_factors, other_factors,
    weight, cotangent, cotangent_in,
    z_out, stats_ref, near_mine, near_other, near_g, z_ref, sem, out_sem,
):
    core = where[0]
    block = 256
    half = z_ref.shape[1]
    nodes = first_mine.shape[0]
    own = pl.ds(pl.multiple_of(core * half, half), half)
    far = pl.ds(pl.multiple_of((1 - core) * half, half), half)

    def loads(k, start, size):
        whole = pl.ds(pl.multiple_of(core * half + start, 256), size)
        part = slice(start, start + size)
        return [
            pltpu.make_async_copy(weight.at[own, whole], near_mine.at[:, part], sem.at[0, k]),
            pltpu.make_async_copy(weight.at[far, whole], near_other.at[:, part], sem.at[1, k]),
        ]

    ranges = ((0, block), (block, half - block))
    copies = [loads(k, *r) for k, r in enumerate(ranges)]
    grads = grad_loads(core, cotangent, cotangent_in, near_g, (0, half), sem.at[2])
    for c in copies[0] + grads + copies[1]:
        c.start()

    def store(j):
        part = slice(2 * j * block, 2 * (j + 1) * block)
        return pltpu.make_async_copy(z_ref.at[:, part], z_out.at[:, part], out_sem.at[j])

    valids = [
        jnp.where(core == k, own_factors[:, 0:1], other_factors[:, 0:1]) for k in range(2)
    ]
    valid = jnp.concatenate(valids, 0)
    for j in range(half // block):
        at = slice(j * block, (j + 1) * block)
        if j < 2:
            for c in copies[j]:
                c.wait()
        for k, (a, b) in enumerate(((first_mine, first_other), (second_mine, second_other))):
            z = mxu(a[...], near_mine[:, at]) + mxu(b[...], near_other[:, at])
            z_ref[k * nodes : (k + 1) * nodes, at] = z + bias[:, at]
        if j == 0:
            for c in grads:
                c.wait()
        if j % 2 == 1:
            store(j // 2).start()
        z = z_ref[:, at]
        sigma = 1.0 / (1.0 + jnp.exp(-z))
        y = z * sigma
        slope = (sigma + y * (1.0 - sigma)) * valid
        g = near_g[:, at].astype(F32) * valid

        def column(x):
            return jnp.sum(x, axis=0, keepdims=True)

        count = jnp.broadcast_to(column(valid), (1, block))
        y_sum = column(y * valid)
        centred = (y - y_sum / jnp.maximum(count, 1.0)) * valid
        stats_ref[0:1, at] = count
        stats_ref[1:2, at] = y_sum
        stats_ref[2:3, at] = column(centred * centred)
        stats_ref[3:4, at] = column(g)
        stats_ref[4:5, at] = column(g * centred)
        stats_ref[5:6, at] = column(slope * g)
        stats_ref[6:7, at] = column(slope)
        stats_ref[7:8, at] = column(slope * centred)
    for j in range(half // block // 2):
        store(j).wait()


def forward(core, mine, other, weight, bias, cotangent, cotangent_in, own, sibling):
    rows, half = cotangent_in.shape
    return call(
        forward_kernel,
        (far_shape((2 * rows, half), F32), shape_of((8, half), F32)),
        "forward",
        in_specs=[SMEM] + [VMEM] * 7 + [HBM] * 3,
        out_specs=(HBM, VMEM),
        scratch_shapes=[
            pltpu.VMEM((half, half), BF),
            pltpu.VMEM((half, half), BF),
            pltpu.VMEM((2 * rows, half), BF),
            pltpu.VMEM((2 * rows, half), F32),
            pltpu.SemaphoreType.DMA((3, 2)),
            pltpu.SemaphoreType.DMA((half // 512,)),
        ],
    )(
        scalars(core), *mine, *other, bias[None, :], own, sibling, weight, cotangent, cotangent_in
    )


def merge_kernel(where, own, received, out):
    upper = where[0] == 1
    a, b = own[...], received[...]
    a, b = jnp.where(upper, b, a), jnp.where(upper, a, b)

    def row(x, k):
        return x[k : k + 1, :]

    na, nb = row(a, 0), row(b, 0)
    n = na + nb
    mean = (row(a, 1) + row(b, 1)) / jnp.maximum(n, 1.0)
    da = row(a, 1) / jnp.maximum(na, 1.0) - mean
    db = row(b, 1) / jnp.maximum(nb, 1.0) - mean
    out[...] = a + b
    out[2:3, :] = (row(a, 2) + na * da * da) + (row(b, 2) + nb * db * db)
    out[4:5, :] = (row(a, 4) + da * row(a, 3)) + (row(b, 4) + db * row(b, 3))
    out[7:8, :] = (row(a, 7) + da * row(a, 6)) + (row(b, 7) + db * row(b, 6))


def merge(own, received, v):
    return call(
        merge_kernel, shape_of(own.shape, F32), "merge", in_specs=[SMEM, VMEM, VMEM]
    )(scalars(v), own, received)


def backward_kernel(
    where, stats_ref, gamma_ref, beta_ref, own_factors, other_factors, z_ref, cotangent, cotangent_in,
    dz_send, dz_keep, dz_scaled, act_first, act_second, vectors, near_z, near_g, sem,
):
    first, core = where[0], where[1]
    rows, half = z_ref.shape
    block = 256
    some = half // block // 2
    nodes = act_first.shape[0]

    def loads(i):
        start = (1 - first if i == 0 else first) * some * block
        part = pl.ds(pl.multiple_of(start, some * block), some * block)
        copy = pltpu.make_async_copy(z_ref.at[:, part], near_z.at[:, part], sem.at[i, 2])
        return [copy] + grad_loads(
            core, cotangent, cotangent_in, near_g, (start, some * block), sem.at[i]
        )

    copies = [loads(i) for i in range(2)]
    for c in copies[0] + copies[1]:
        c.start()
    valids, inverses = (
        jnp.concatenate(
            [
                jnp.where(core == k, own_factors[:, lane : lane + 1], other_factors[:, lane : lane + 1])
                for k in range(2)
            ],
            0,
        )
        for lane in range(2)
    )

    def columns(i, k, out):
        base = ((1 - first if i == 0 else first) * some + k) * block
        at = pl.ds(pl.multiple_of(base, block), block)
        vector = pl.ds(pl.multiple_of(core * half + base, block), block)
        z = near_z[:, at]
        valid = valids
        stats = stats_ref[:, at]
        gamma, beta = gamma_ref[:, vector], beta_ref[:, vector]
        n = stats[0:1, :]
        mean = stats[1:2, :] / n
        deviation = lax.rsqrt(stats[2:3, :] / n + 1e-05)
        shift = stats[3:4, :]
        scale = deviation * stats[4:5, :]
        gain = gamma * deviation
        vectors[0:1, at] = gain * (
            stats[5:6, :] - shift / n * stats[6:7, :] - deviation * scale / n * stats[7:8, :]
        )
        vectors[1:2, at] = scale
        vectors[2:3, at] = shift
        vectors[3:8, at] = jnp.zeros((5, block), F32)
        sigma = 1.0 / (1.0 + jnp.exp(-z))
        y = z * sigma
        slope = (sigma + y * (1.0 - sigma)) * valid
        g = near_g[:, at].astype(F32) * valid
        normalized = (y - mean) * deviation
        act = (valid * (gamma * normalized + beta)).astype(BF)
        act_first[:, at] = act[:nodes]
        act_second[:, at] = act[nodes:]
        dz = gain * (g - shift / n - normalized * (scale / n)) * slope
        dz_scaled[:, at] = (dz * inverses).astype(BF)
        out[:, k * block : (k + 1) * block] = dz.astype(BF)

    for i, out in enumerate((dz_send, dz_keep)):
        for c in copies[i]:
            c.wait()
        for k in range(some):
            columns(i, k, out)


def backward(core, first, z, stats, gamma, beta, cotangent, cotangent_in, own, sibling):
    rows, half = z.shape
    return call(
        backward_kernel,
        (
            shape_of((rows, half // 2), BF),
            shape_of((rows, half // 2), BF),
            shape_of((rows, half), BF),
            shape_of((rows // 2, half), BF),
            shape_of((rows // 2, half), BF),
            shape_of((8, half), F32),
        ),
        "backward",
        in_specs=[SMEM] + [VMEM] * 5 + [HBM] * 3,
        scratch_shapes=[
            pltpu.VMEM((rows, half), F32),
            pltpu.VMEM((rows, half), BF),
            pltpu.SemaphoreType.DMA((2, 3)),
        ],
    )(
        scalars(first, core), stats, gamma[None, :], beta[None, :], own, sibling, z, cotangent, cotangent_in
    )


def weight_part_kernel(t, where, *refs):
    aggs, (dz, dz_pair, out, near, sem) = refs[:8], refs[8:]
    nodes = aggs[0].shape[0]
    columns = slice(t * out.shape[0], (t + 1) * out.shape[0])

    def copy(k, pair):
        return pltpu.make_async_copy(aggs[2 * pair + k % 2 + 4 * (k // 2)].at[:, columns], near.at[k], sem.at[k])

    for flag, pair in ((1, 0), (0, 1)):

        @pl.when(where[0] == flag)
        def _():
            for k in range(4):
                copy(k, pair).start()

    total = 0.0
    for k in range(4):
        copy(k, 0).wait()
        rows = slice(k % 2 * nodes, (k % 2 + 1) * nodes)
        total = total + by_rows(near[k], (dz, dz_pair)[k // 2][rows, :])
    out[...] = total.astype(BF)


def weight_part(flag, aggs, dz, dz_pair, t):
    nodes, half = aggs[0].shape
    tall = half // TILES
    return call(
        functools.partial(weight_part_kernel, t),
        shape_of((tall, dz.shape[1]), BF),
        "weight_part",
        in_specs=[SMEM] + [HBM] * 8 + [VMEM] * 2,
        scratch_shapes=[pltpu.VMEM((4, nodes, tall), BF), pltpu.SemaphoreType.DMA((4,))],
    )(scalars(flag), *aggs, dz, dz_pair)


def fold_kernel(where, own, received, away, keep):
    rows = keep.shape[0]
    for side, out in ((1 - where[0], away), (where[0], keep)):
        part = pl.ds(pl.multiple_of(side * rows, rows), rows)
        out[...] = (own[part, :].astype(F32) + received[part, :].astype(F32)).astype(BF)


def fold(own, received, v):
    rows, w = own.shape
    out = shape_of((rows // 2, w), BF)
    return call(fold_kernel, (out, out), "fold", in_specs=[SMEM, VMEM, VMEM])(
        scalars(v), own, received
    )


def total_kernel(own, received, out):
    out[...] = (own[...].astype(F32) + received[...].astype(F32)).astype(BF)


def total_of(own, received):
    return call(total_kernel, shape_of(own.shape, BF), "total")(own, received)


def join_kernel(where, own, received, out):
    rows = own.shape[0]
    for side, x in ((where[0], own), (1 - where[0], received)):
        out[pl.ds(pl.multiple_of(side * rows, rows), rows), :] = x[...]


def join(own, received, v):
    rows, w = own.shape
    return call(join_kernel, shape_of((2 * rows, w), BF), "join", in_specs=[SMEM, VMEM, VMEM])(
        scalars(v), own, received
    )


def place_kernel(n, where, *refs):
    pieces, (out, wide, put) = refs[:n], refs[-3:]

    def write(i):
        rows, w = pieces[i].shape
        row = pl.multiple_of(where[2 * i], 256)
        column = pl.multiple_of(where[2 * i + 1], 128)
        return pltpu.make_async_copy(
            wide.at[i], out.at[pl.ds(row, rows), pl.ds(column, w)], put.at[i]
        )

    for i in range(n):
        step = 128

        @pl.loop(0, pieces[i].shape[0] // step)
        def _(k):
            part = pl.ds(pl.multiple_of(k * step, step), step)
            wide[i, part, :] = pieces[i][part, :].astype(F32)

        write(i).start()
    for i in range(n):
        write(i).wait()


def place(total, pieces, shape, cost=FREE):
    n = len(pieces)
    rows, w = pieces[0][0].shape
    operands = [scalars(*[x for p in pieces for x in p[1:]])] + [p[0] for p in pieces]
    specs = [SMEM] + [VMEM] * n
    aliases = {}
    if total is not None:
        aliases = {len(operands): 0}
        operands.append(total)
        specs.append(HBM)
    return call(
        functools.partial(place_kernel, n),
        far_shape(shape, F32),
        "place",
        in_specs=specs,
        out_specs=HBM,
        cost=cost,
        scratch_shapes=[pltpu.VMEM((n, rows, w), F32), pltpu.SemaphoreType.DMA((n,))],
        input_output_aliases=aliases,
    )(*operands)


def back_part_kernel(columns, where, own, sibling, dz, out):
    nodes = own.shape[0]
    total = 0.0
    for side, count in ((where[0], own), (1 - where[0], sibling)):
        rows = pl.ds(pl.multiple_of(side * nodes, nodes), nodes)
        total = total + by_rows(count[:, columns], dz[rows, :])
    out[...] = total.astype(BF)


def back_part(core, own, sibling, dz, k, parts):
    rows = own.shape[1] // parts
    return call(
        functools.partial(back_part_kernel, slice(k * rows, (k + 1) * rows)),
        shape_of((rows, dz.shape[1]), BF),
        "back_part",
        in_specs=[SMEM] + [VMEM] * 3,
    )(scalars(core), own, sibling, dz)


def halve_kernel(own, received, away, keep):
    rows = keep.shape[0]
    keep[...] = (own[:rows].astype(F32) + received[:rows].astype(F32)).astype(BF)
    away[...] = (own[rows:].astype(F32) + received[rows:].astype(F32)).astype(BF)


def halve(own, received):
    rows, w = own.shape
    out = shape_of((rows // 2, w), BF)
    return call(halve_kernel, (out, out), "halve")(own, received)


def own_back_body(where, own, sibling, dz, act_first, act_second, keep, away, act_keep, act_away):
    nodes = keep.shape[0]
    core = where[0]
    for side, count, out in ((core, own, keep), (1 - core, sibling, away)):
        part = pl.ds(pl.multiple_of(side * nodes, nodes), nodes)
        out[...] = by_rows(count[...], dz[part, :]).astype(BF)
    act_keep[...] = jnp.where(core == 0, act_first[...], act_second[...])
    act_away[...] = jnp.where(core == 0, act_second[...], act_first[...])


def own_back(core, own, sibling, dz, act_first, act_second):
    nodes, half = act_first.shape
    out, far = shape_of((nodes, half), BF), shape_of((nodes, half), BF)
    return call(own_back_body, (far, out, far, out), "own_back", in_specs=[SMEM] + [VMEM] * 5)(
        scalars(core), own, sibling, dz, act_first, act_second
    )


def finish_kernel(
    where, rows, back, back_in, vec, vec_in, own, own_in, act, act_in, weight,
    grad, activations, vectors, near_weight, near_own, table, weight_sem, own_sem, act_sem,
):
    core = where[0]
    nodes, half = own.shape
    sends = rows.shape[0]
    block = 256
    blocks = weight.shape[0] // block

    def side_of(k):
        return pl.ds(pl.multiple_of((core if k == 0 else 1 - core) * half, half), half)

    owns = [
        pltpu.make_async_copy(x, near_own.at[k], own_sem.at[k]) for k, x in enumerate((own, own_in))
    ]
    acts = [
        pltpu.make_async_copy(x, activations.at[:, side_of(k)], act_sem.at[k])
        for k, x in enumerate((act, act_in))
    ]
    weights = [
        pltpu.make_async_copy(
            weight.at[k * block : (k + 1) * block, :],
            near_weight.at[k * block : (k + 1) * block, :],
            weight_sem.at[k],
        )
        for k in range(blocks)
    ]
    for c in owns + weights + acts:
        c.start()
    hot = (rows[...] == lax.broadcasted_iota(jnp.int32, (sends, nodes), 1)).astype(BF)
    for k, (back_part, vector) in enumerate(((back[:sends], vec), (back_in[...], vec_in))):
        vectors[:, side_of(k)] = vector[...]
        owns[k].wait()
        part = near_own[k].astype(F32) + by_rows(hot, back_part)
        table[:, side_of(k)] = part.astype(BF)
    for k in range(blocks):
        weights[k].wait()
        part = slice(k * block, (k + 1) * block)
        grad[:, part] = lax.dot_general(
            table[...], near_weight[part, :], (((1,), (1,)), ((), ())), preferred_element_type=F32
        ).astype(BF)
    for c in acts:
        c.wait()


def finish(core, rows, back, back_in, own, own_in, act, act_in, vec, vec_in, weight):
    nodes, half = own.shape
    width = 2 * half
    return call(
        finish_kernel,
        (
            shape_of((nodes, width), BF),
            shape_of((nodes, width), BF),
            shape_of((8, width), F32),
        ),
        "finish",
        in_specs=[SMEM] + [VMEM] * 5 + [HBM] * 5,
        out_specs=(VMEM, VMEM, VMEM),
        scratch_shapes=[
            pltpu.VMEM(weight.shape, BF),
            pltpu.VMEM((2, nodes, half), BF),
            pltpu.VMEM((nodes, width), BF),
            pltpu.SemaphoreType.DMA((width // 256,)),
            pltpu.SemaphoreType.DMA((2,)),
            pltpu.SemaphoreType.DMA((2,)),
        ],
    )(scalars(core), rows, back, back_in, vec, vec_in, own, own_in, act, act_in, weight)


def on_device(
    size,
    features,
    weight,
    bias,
    gamma,
    beta,
    neighbours,
    edge_mask,
    node_mask,
    send_rows,
    send_mask,
    cotangent,
):
    nodes, width = features.shape
    sends = send_rows.shape[0]
    half = width // 2
    quarter = width // 4
    rest = list(range(3, size.bit_length() - 1))
    levels = len(rest)
    cut = (levels + 1) // 2
    ways = {"f": ["f"], "s": ["s"], "z0": rest[:cut], "z1": rest[cut:]}

    me = lax.axis_index("dom")
    core = me & 1
    is0 = core == 0
    b1, b2 = (me >> 1) & 1, (me >> 2) & 1
    first = jnp.where(is0, b1, b2)
    second = jnp.where(is0, b2, b1)
    first_weight = jnp.where(is0, 2, 4)
    second_weight = 6 - first_weight

    def bit(b):
        return first if b == "f" else second if b == "s" else (me >> b) & 1

    def weight_of(b):
        return first_weight if b == "f" else second_weight if b == "s" else 1 << b

    def peer(i, b):
        if b == "f":
            return i ^ (4 if i & 1 else 2)
        if b == "s":
            return i ^ (2 if i & 1 else 4)
        return i ^ (1 << b)

    def along(x, b):
        return lax.ppermute(x, "dom", [(i, peer(i, b)) for i in range(size)])

    def swap(x):
        return lax.ppermute(x, "dom", [(i, i ^ 1) for i in range(size)])

    token = [jnp.zeros((8, 128), F32)]

    def arrive(*x):
        *x, token[0] = lax.optimization_barrier((*x, token[0]))
        return x[0] if len(x) == 1 else x

    def start(generators):
        running = dict(generators)
        for k in running:
            next(running[k])
        done = {}

        def advance(k):
            try:
                next(running[k])
            except StopIteration as stop:
                done[k] = stop.value

        return advance, done

    def bits_of(way):
        return [b for name in way.split() for b in ways[name]]

    live_row = jnp.where(send_mask > 0, send_rows, -1)[:, None]
    out_away, *out_keep = outgoing_rows(
        core, live_row, features, tuple(w for w, _ in HALO_WAYS)
    )
    outgoing = stack(out_keep, arrive(swap(out_away)))
    axes = bits_of(BACK_WAY)
    halo_rows = sends * size
    chip_rows = 2 * sends

    def gather_halo(x, way):
        got = []
        for b in bits_of(way):
            received = along(x, b)
            yield
            outer = 1 << len([g for g in got if axes.index(g) < axes.index(b)])
            x = interleave(x, arrive(received), outer)
            got.append(b)
        return x

    generators = {
        k: gather_halo(x, way) for k, (x, (_, way)) in enumerate(zip(outgoing, HALO_WAYS))
    }
    advance, halo = start(generators)

    def hop():
        for k in generators:
            advance(k)

    live_neighbour = jnp.where(edge_mask > 0, neighbours, -1)
    packed = jnp.concatenate([live_neighbour, node_mask[:, None]], 1)
    place_of = jnp.arange(halo_rows)
    chip, row = place_of // chip_rows, place_of % chip_rows
    relative = 0
    for k, b in enumerate(axes):
        relative = relative + ((chip >> (len(axes) - 1 - k)) & 1) * weight_of(b)
    owner = (me ^ relative) ^ (row // sends)
    label = (nodes + owner * sends + row % sends)[None, :]
    packed, label = arrive(packed, label)
    sibling_packed = arrive(swap(packed))
    hop()
    feature_out, cotangent_out = arrive(*split(core, *arrive(features, cotangent)))
    feature_in, cotangent_in = swap(feature_out), swap(cotangent_out)
    packed = arrive(packed)
    own = arrive(*counts(packed, label))
    hop()
    feature_in, cotangent_in, sibling_packed = arrive(feature_in, cotangent_in, sibling_packed)
    sibling = arrive(*counts(sibling_packed, label))
    hop()
    for _ in range(levels - 1):
        hop()

    agg_mine = aggregate(
        core, features, feature_in, own, sibling, [halo[k] for k in generators]
    )
    agg_other = [swap(x) for x in agg_mine]
    mine_pair = [along(x, "f") for x in agg_mine]
    agg_other = [arrive(x) for x in agg_other]
    other_pair = [along(x, "f") for x in agg_other]
    own_bias = lax.dynamic_slice_in_dim(bias, core * half, half, 0)
    z, stats = forward(
        core, agg_mine, agg_other, weight, own_bias, cotangent, cotangent_in, own[2], sibling[2]
    )

    same = (second == core).astype(jnp.int32)
    for k, b in enumerate(bits_of("z1 z0 s f")):
        received = along(stats, b)
        if k == 0:
            mine_pair = [arrive(x) for x in mine_pair]
        if b == "s":
            other_pair = [arrive(x) for x in other_pair]
        stats = merge(stats, arrive(received), bit(b))
    dz_send, dz_keep, dz_scaled, act_first, act_second, vectors = backward(
        core, first, z, stats, gamma, beta, cotangent, cotangent_in, own[2], sibling[2]
    )

    dz_pair = along(dz_send, "f")
    dz_keep, dz_scaled = arrive(dz_keep, dz_scaled)
    aggs = [*agg_mine, *agg_other, *mine_pair, *other_pair]
    dz_pair = arrive(dz_pair)

    def weight_gradient(t):
        received = along(weight_part(1 - same, aggs, dz_keep, dz_pair, t), "s")
        part = weight_part(same, aggs, dz_keep, dz_pair, t)
        yield
        part = arrive(part)
        if t == 0:
            yield
        received = arrive(received)
        for b in rest:
            out, part = fold(part, received, bit(b))
            received = along(out, b)
            yield
            received = arrive(received)
        part = total_of(part, received)
        for b in reversed(rest):
            received = along(part, b)
            yield
            part = join(part, arrive(received), bit(b))
        return part

    def reduce_halo():
        received, part = along(back_send, axes[0]), back_keep
        for b in axes[1:]:
            yield
            out, part = halve(part, arrive(received))
            received = along(out, b)
        yield
        return total_of(part, arrive(received))

    advance, weight_parts = start({t: weight_gradient(t) for t in range(TILES)})

    def step():
        for t in range(TILES):
            advance(t)

    for t in range(TILES):
        advance(t)
    back_send, back_keep = (
        back_part(core, own[0], sibling[0], dz_scaled, k, 2) for k in (1, 0)
    )
    kept_back, away_back, act, act_away = own_back(
        core, own[1], sibling[1], dz_scaled, act_first, act_second
    )
    back_send, back_keep, kept_back, away_back, act, act_away = arrive(
        back_send, back_keep, kept_back, away_back, act, act_away
    )
    own_in, act_in, vectors_in = swap(away_back), swap(act_away), swap(vectors)
    advance(0)
    back_send = arrive(back_send)
    advance_halo, halo_part = start({"h": reduce_halo()})
    own_in, act_in, vectors_in = arrive(own_in, act_in, vectors_in)
    for k in range(levels):
        step()
        if k < 2:
            advance_halo("h")
    for k in range(levels):
        step()
    for _ in ways["z0"]:
        advance_halo("h")

    tall = half // TILES
    tiles = range(TILES)
    part = [weight_parts[t] for t in tiles]
    across = [along(x, "s") for x in part]
    pair = [along(x, "f") for x in part]
    here = [swap(x) for x in part]
    here_at, there_at = core * half, (1 - core) * half
    shape = (width, width)

    def pieces(own, sibling, row, sibling_row, column, sibling_column):
        return [(x, row * half + t * tall, here_at + column * quarter) for t, x in own.items()] + [
            (x, sibling_row * half + t * tall, there_at + sibling_column * quarter)
            for t, x in sibling.items()
        ]

    def numbered(x):
        return dict(enumerate(x))

    pair_across, here_across, here_pair = [], [], []
    for t in tiles:
        across[t] = arrive(across[t])
        pair_across.append(along(across[t], "f"))
        here_across.append(swap(across[t]))
        pair[t] = arrive(pair[t])
        here_pair.append(swap(pair[t]))
        if t == 0:
            here = [arrive(x) for x in here]
            total = place(
                None, pieces(numbered(part), numbered(here), second, first, first, second), shape, SMALL
            )
            total = arrive(total)
    while "h" not in halo_part:
        advance_halo("h")
    back = halo_part["h"]
    back_in = arrive(swap(back[sends:]))
    grad_features, activations, vectors = finish(
        core, live_row, back, back_in, kept_back, own_in, act, act_in, vectors, vectors_in, weight
    )
    grad_features, activations, vectors = arrive(grad_features, activations, vectors)
    here_across = [arrive(x) for x in here_across]
    here_pair = [arrive(x) for x in here_pair]
    total = place(
        total,
        pieces(numbered(across), numbered(here_across), 1 - second, 1 - first, first, second)
        + pieces(numbered(pair), numbered(here_pair), second, first, 1 - first, 1 - second),
        shape,
    )
    total = arrive(total)
    for t in tiles:
        pair_across[t] = arrive(pair_across[t])
        here_pair_across = swap(pair_across[t])
        total = place(
            total,
            pieces(
                {t: pair_across[t]},
                {t: here_pair_across},
                1 - second,
                1 - first,
                1 - first,
                1 - second,
            ),
            shape,
            SMALL,
        )
        if t == 0:
            total = arrive(total)
            vectors = vectors + token[0][0, 0]
    return activations, grad_features, total, vectors[0], vectors[1], vectors[2]


def solution(mesh):
    size = mesh.shape["dom"]
    return jax.shard_map(
        functools.partial(on_device, size),
        mesh=mesh,
        in_specs=(
            P("dom", None),
            P(),
            P(),
            P(),
            P(),
            P("dom", None),
            P("dom", None),
            P("dom"),
            P("dom"),
            P("dom"),
            P("dom", None),
        ),
        out_specs=(P("dom", None), P("dom", None), P(), P(), P(), P()),
        check_vma=False,
    )
```

```python
import functools

import jax
import jax.numpy as jnp
from jax import lax
from jax.experimental import pallas as pl
from jax.experimental.pallas import tpu as pltpu
from jax.sharding import PartitionSpec as P

BF = jnp.bfloat16
F32 = jnp.float32
MIB = 1 << 20
HALO_WIDTHS = (512, 512)
TILES = 2
LAST = ("q", "p")
ORDER = "K O d0 d1 G d0 d1 H B d0 d1 t h d0 d1 b t h d0 d1 t h e t h x0 x1 p0 p1 t R F P"

FREE = pl.CostEstimate(flops=0, bytes_accessed=0, transcendentals=0)
LARGE = pl.CostEstimate(flops=5_000_000_000, bytes_accessed=0, transcendentals=0)
SMALL = pl.CostEstimate(flops=0, bytes_accessed=0, transcendentals=0)
HBM = pl.BlockSpec(memory_space=pltpu.HBM)
SMEM = pl.BlockSpec(memory_space=pltpu.SMEM)
VMEM = pl.BlockSpec(memory_space=pltpu.VMEM)
BY_ROWS = (((0,), (0,)), ((), ()))


def shape_of(shape, dtype):
    return jax.ShapeDtypeStruct(shape, dtype)


def far_shape(shape, dtype):
    return pltpu.HBM(shape, dtype)


def call(body, out_shape, name, vmem=24, cost=FREE, **rest):
    kernel = pl.pallas_call(
        body,
        out_shape=out_shape,
        compiler_params=pltpu.CompilerParams(vmem_limit_bytes=vmem * MIB),
        cost_estimate=cost,
        name=name,
        **rest,
    )
    specs = rest.get("in_specs")

    def run(*operands):
        if specs is None:
            return kernel(*operands)
        return kernel(
            *[
                pltpu.with_memory_space_constraint(x, pltpu.HBM) if spec is HBM else x
                for x, spec in zip(operands, specs)
            ]
        )

    return run


def scalars(*x):
    return jnp.stack([jnp.int32(v) for v in x])


def mxu(a, b):
    return jnp.dot(a, b, preferred_element_type=F32)


def by_rows(a, b):
    return lax.dot_general(a, b, BY_ROWS, preferred_element_type=F32)


def copy_all(copies):
    for c in copies:
        c.start()
    for c in copies:
        c.wait()


def tick_kernel(x, out):
    out[...] = x[...]


def tick_of(x):
    return call(tick_kernel, shape_of(x.shape, x.dtype), "tick", cost=LARGE)(x)


def outgoing_kernel(where, rows, features, away, *keep):
    nodes, width = features.shape
    half = width // 2
    hot = (rows[...] == lax.broadcasted_iota(jnp.int32, (rows.shape[0], nodes), 1)).astype(BF)
    there = features[:, pl.ds(pl.multiple_of((1 - where[0]) * half, half), half)]
    away[...] = mxu(hot, there).astype(BF)
    here = mxu(hot, features[:, pl.ds(pl.multiple_of(where[0] * half, half), half)]).astype(BF)
    at = 0
    for out in keep:
        out[...] = here[:, at : at + out.shape[1]]
        at += out.shape[1]


def outgoing_rows(core, rows, features, widths):
    sends, half = rows.shape[0], features.shape[1] // 2
    return call(
        outgoing_kernel,
        tuple(shape_of((sends, w), BF) for w in (half,) + widths),
        "outgoing",
        in_specs=[SMEM, VMEM, VMEM],
    )(scalars(core), rows, features)


def stack_kernel(n, received, *refs):
    own, outs = refs[:n], refs[n:]
    at = 0
    for x, out in zip(own, outs):
        rows, w = x.shape
        out[:rows, :] = x[...]
        out[rows:, :] = received[:, at : at + w]
        at += w


def stack(own, received):
    return call(
        functools.partial(stack_kernel, len(own)),
        tuple(shape_of((2 * x.shape[0], x.shape[1]), BF) for x in own),
        "stack",
    )(received, *own)


def stack_rows_kernel(own, received, out):
    rows = own.shape[0]
    out[:rows, :] = own[...]
    out[rows:, :] = received[...]


def stack_rows(own, received, cost=FREE):
    rows, w = own.shape
    return call(stack_rows_kernel, shape_of((2 * rows, w), own.dtype), "stack_rows", cost=cost)(
        own, received
    )


def counts_kernel(packed, label, halo_count, own_count, factors):
    nodes, columns = packed.shape
    slots = columns - 1

    def count(labels):
        total = jnp.zeros((nodes, labels.shape[1]), F32)
        for e in range(slots):
            total = total + jnp.where(packed[:, e : e + 1] == labels, 1.0, 0.0)
        return total

    halo_count[...] = count(label[...]).astype(BF)
    local = lax.broadcasted_iota(jnp.int32, (nodes, nodes), 1)
    row = lax.broadcasted_iota(jnp.int32, (nodes, nodes), 0)
    own_count[...] = (count(local) + jnp.where(row == local, 2.0, 0.0)).astype(BF)
    degree = jnp.zeros((nodes, 1), F32)
    for e in range(slots):
        degree = degree + jnp.where(packed[:, e : e + 1] >= 0, 1.0, 0.0)
    lane = lax.broadcasted_iota(jnp.int32, factors.shape, 1)
    factors[...] = jnp.where(lane == 0, packed[:, slots:].astype(F32), 1.0 / (degree + 1.0))


def counts(packed, label):
    nodes = packed.shape[0]
    return call(
        counts_kernel,
        (
            shape_of((nodes, label.shape[1]), BF),
            shape_of((nodes, nodes), BF),
            shape_of((nodes, 128), F32),
        ),
        "counts",
    )(packed, label)


def aggregate_kernel(n, where, features, features_in, *refs):
    own, sibling, halos = refs[:3], refs[3:6], refs[6 : 6 + n]
    out, near, sem = refs[6 + n :]
    _, nodes, half = near.shape
    core = where[0]
    here = pl.ds(pl.multiple_of(core * half, half), half)
    copies = [
        pltpu.make_async_copy(x.at[:, here], near.at[k], sem.at[k])
        for k, x in enumerate((features, features_in))
    ]
    for c in copies:
        c.start()
    for k, (halo_count, own_count, factors) in enumerate((own, sibling)):
        rows = pl.ds(pl.multiple_of((core if k == 0 else 1 - core) * nodes, nodes), nodes)
        start = 0
        for i, halo in enumerate(halos):
            part = slice(start, start + halo.shape[1])
            total = mxu(halo_count[...], halo[...])
            if i == 0:
                copies[k].wait()
            total = total + mxu(own_count[...], near[k][:, part])
            out[rows, part] = (total * factors[:, 1:2]).astype(BF)
            start += halo.shape[1]


def aggregate(core, features, features_in, own, sibling, halos):
    rows, width = features.shape
    half = width // 2
    return call(
        functools.partial(aggregate_kernel, len(halos)),
        shape_of((2 * rows, half), BF),
        "aggregate",
        in_specs=[SMEM, HBM, HBM] + [VMEM] * (6 + len(halos)),
        scratch_shapes=[pltpu.VMEM((2, rows, half), BF), pltpu.SemaphoreType.DMA((2,))],
    )(scalars(core), features, features_in, *own, *sibling, *halos)


def grad_loads(core, cotangent, cotangent_in, near_g, column, sems):
    rows, width = cotangent.shape
    start, size = column
    whole = pl.ds(pl.multiple_of(core * (width // 2) + start, 256), size)
    own = pl.ds(pl.multiple_of(core * rows, rows), rows)
    far = pl.ds(pl.multiple_of((1 - core) * rows, rows), rows)
    return [
        pltpu.make_async_copy(cotangent.at[:, whole], near_g.at[own, :], sems.at[0]),
        pltpu.make_async_copy(cotangent_in.at[:, whole], near_g.at[far, :], sems.at[1]),
    ]


def factor(core, own, other, lane):
    return jnp.concatenate(
        [jnp.where(core == k, own[:, lane : lane + 1], other[:, lane : lane + 1]) for k in range(2)], 0
    )


def forward_kernel(
    where, mine, other, constants, own_factors, other_factors,
    weight, cotangent, cotangent_in,
    z_out, stats_ref, near_mine, near_other, near_g, z_ref, sem, out_sem,
):
    core = where[0]
    block = 256
    half = z_ref.shape[1]
    own = pl.ds(pl.multiple_of(core * half, half), half)
    far = pl.ds(pl.multiple_of((1 - core) * half, half), half)

    def loads(k, start, size):
        whole = pl.ds(pl.multiple_of(core * half + start, 256), size)
        part = slice(start, start + size)
        return [
            pltpu.make_async_copy(weight.at[own, whole], near_mine.at[:, part], sem.at[0, k]),
            pltpu.make_async_copy(weight.at[far, whole], near_other.at[:, part], sem.at[1, k]),
        ]

    ranges = ((0, block), (block, half - block))
    copies = [loads(k, *r) for k, r in enumerate(ranges)]
    grads = grad_loads(core, cotangent, cotangent_in, near_g, (0, half), sem.at[2])
    for c in copies[0] + grads + copies[1]:
        c.start()

    def store(j):
        part = slice(2 * j * block, 2 * (j + 1) * block)
        return pltpu.make_async_copy(z_ref.at[:, part], z_out.at[:, part], out_sem.at[j])

    valid = factor(core, own_factors, other_factors, 0)
    bias = constants[0:1, own]
    for j in range(half // block):
        at = slice(j * block, (j + 1) * block)
        if j < 2:
            for c in copies[j]:
                c.wait()
        z_ref[:, at] = (
            mxu(mine[...], near_mine[:, at]) + mxu(other[...], near_other[:, at]) + bias[:, at]
        )
        if j == 0:
            for c in grads:
                c.wait()
        if j % 2 == 1:
            store(j // 2).start()
        z = z_ref[:, at]
        sigma = 1.0 / (1.0 + jnp.exp(-z))
        y = z * sigma
        slope = (sigma + y * (1.0 - sigma)) * valid
        g = near_g[:, at].astype(F32) * valid

        def column(x):
            return jnp.sum(x, axis=0, keepdims=True)

        count = jnp.broadcast_to(column(valid), (1, block))
        y_sum = column(y * valid)
        centred = (y - y_sum / jnp.maximum(count, 1.0)) * valid
        stats_ref[0:1, at] = count
        stats_ref[1:2, at] = y_sum
        stats_ref[2:3, at] = column(centred * centred)
        stats_ref[3:4, at] = column(g)
        stats_ref[4:5, at] = column(g * centred)
        stats_ref[5:6, at] = column(slope * g)
        stats_ref[6:7, at] = column(slope)
        stats_ref[7:8, at] = column(slope * centred)
    for j in range(half // block // 2):
        store(j).wait()


def forward(core, mine, other, weight, constants, cotangent, cotangent_in, own, sibling):
    rows, half = cotangent.shape[0], mine.shape[1]
    return call(
        forward_kernel,
        (far_shape((2 * rows, half), F32), shape_of((8, half), F32)),
        "forward",
        in_specs=[SMEM] + [VMEM] * 5 + [HBM] * 3,
        out_specs=(HBM, VMEM),
        scratch_shapes=[
            pltpu.VMEM((half, half), BF),
            pltpu.VMEM((half, half), BF),
            pltpu.VMEM((2 * rows, half), BF),
            pltpu.VMEM((2 * rows, half), F32),
            pltpu.SemaphoreType.DMA((3, 2)),
            pltpu.SemaphoreType.DMA((half // 512,)),
        ],
    )(
        scalars(core), mine, other, constants, own, sibling, weight, cotangent, cotangent_in
    )


def merge_kernel(where, own, received, out):
    upper = where[0] == 1
    a, b = own[...], received[...]
    a, b = jnp.where(upper, b, a), jnp.where(upper, a, b)

    def row(x, k):
        return x[k : k + 1, :]

    na, nb = row(a, 0), row(b, 0)
    n = na + nb
    mean = (row(a, 1) + row(b, 1)) / jnp.maximum(n, 1.0)
    da = row(a, 1) / jnp.maximum(na, 1.0) - mean
    db = row(b, 1) / jnp.maximum(nb, 1.0) - mean
    out[...] = a + b
    out[2:3, :] = (row(a, 2) + na * da * da) + (row(b, 2) + nb * db * db)
    out[4:5, :] = (row(a, 4) + da * row(a, 3)) + (row(b, 4) + db * row(b, 3))
    out[7:8, :] = (row(a, 7) + da * row(a, 6)) + (row(b, 7) + db * row(b, 6))


def merge(own, received, v):
    return call(
        merge_kernel, shape_of(own.shape, F32), "merge", in_specs=[SMEM, VMEM, VMEM]
    )(scalars(v), own, received)


def gradient(where, at, stats_ref, constants, z, g_in, valid):
    core, half, start = where
    size = z.shape[1]
    vector = pl.ds(pl.multiple_of(core * half + start, size), size)
    stats = stats_ref[:, at]
    gamma, beta = constants[1:2, vector], constants[2:3, vector]
    n = stats[0:1, :]
    mean = stats[1:2, :] / n
    deviation = lax.rsqrt(stats[2:3, :] / n + 1e-05)
    shift = stats[3:4, :]
    scale = deviation * stats[4:5, :]
    gain = gamma * deviation
    vectors = (
        gain * (stats[5:6, :] - shift / n * stats[6:7, :] - deviation * scale / n * stats[7:8, :]),
        scale,
        shift,
    )
    sigma = 1.0 / (1.0 + jnp.exp(-z))
    y = z * sigma
    slope = (sigma + y * (1.0 - sigma)) * valid
    g = g_in.astype(F32) * valid
    normalized = (y - mean) * deviation
    dz = gain * (g - shift / n - normalized * (scale / n)) * slope
    return dz, valid * (gamma * normalized + beta), vectors


def dz_kernel(
    where, stats_ref, constants, own_factors, other_factors, z_ref, cotangent, cotangent_in,
    out, near_z, near_g, sem,
):
    side, core = where[0], where[1]
    half, size = z_ref.shape[1], out.shape[1]
    block = 256
    blocks = size // block

    def loads(k):
        start = side * size + k * block
        part = pl.ds(pl.multiple_of(start, block), block)
        here = slice(k * block, (k + 1) * block)
        copy = pltpu.make_async_copy(z_ref.at[:, part], near_z.at[:, here], sem.at[k, 2])
        return [copy] + grad_loads(
            core, cotangent, cotangent_in, near_g.at[:, here], (start, block), sem.at[k]
        )

    copies = [loads(k) for k in range(blocks)]
    for c in copies[0] + copies[1]:
        c.start()
    valid = factor(core, own_factors, other_factors, 0)
    for k in range(blocks):
        for c in copies[k]:
            c.wait()
        here = slice(k * block, (k + 1) * block)
        start = side * size + k * block
        at = pl.ds(pl.multiple_of(start, block), block)
        dz, _, _ = gradient(
            (core, half, start), at, stats_ref, constants, near_z[:, here], near_g[:, here], valid
        )
        out[:, here] = dz.astype(BF)


def dz_of(core, side, z, stats, constants, cotangent, cotangent_in, own, sibling):
    rows, half = z.shape
    return call(
        dz_kernel,
        shape_of((rows, half // 2), BF),
        "dz",
        in_specs=[SMEM] + [VMEM] * 4 + [HBM] * 3,
        scratch_shapes=[
            pltpu.VMEM((rows, half // 2), F32),
            pltpu.VMEM((rows, half // 2), BF),
            pltpu.SemaphoreType.DMA((2, 3)),
        ],
    )(scalars(side, core), stats, constants, own, sibling, z, cotangent, cotangent_in)


def outputs_kernel(
    where, stats_ref, constants, own_factors, other_factors, z_ref, cotangent, cotangent_in,
    dz_scaled, act_keep, act_away, vectors, near_z, near_g, sem,
):
    core = where[0]
    rows, half = z_ref.shape
    nodes = rows // 2
    block = 256
    copies = [pltpu.make_async_copy(z_ref, near_z, sem.at[2])]
    copies += grad_loads(core, cotangent, cotangent_in, near_g, (0, half), sem)
    for c in copies:
        c.start()
    valid, inverse = (factor(core, own_factors, other_factors, lane) for lane in range(2))
    for c in copies:
        c.wait()
    vectors[3:8, :] = jnp.zeros((5, half), F32)
    for k in range(half // block):
        at = slice(k * block, (k + 1) * block)
        dz, act, sums = gradient(
            (core, half, k * block), at, stats_ref, constants, near_z[:, at], near_g[:, at], valid
        )
        dz_scaled[:, at] = (dz * inverse).astype(BF)
        act = act.astype(BF)
        act_keep[:, at] = jnp.where(core == 0, act[:nodes], act[nodes:])
        act_away[:, at] = jnp.where(core == 0, act[nodes:], act[:nodes])
        for i, x in enumerate(sums):
            vectors[i : i + 1, at] = x


def outputs(core, z, stats, constants, cotangent, cotangent_in, own, sibling):
    rows, half = z.shape
    act = shape_of((rows // 2, half), BF)
    return call(
        outputs_kernel,
        (shape_of((rows, half), BF), act, act, shape_of((8, half), F32)),
        "outputs",
        in_specs=[SMEM] + [VMEM] * 4 + [HBM] * 3,
        scratch_shapes=[
            pltpu.VMEM((rows, half), F32),
            pltpu.VMEM((rows, half), BF),
            pltpu.SemaphoreType.DMA((3,)),
        ],
    )(scalars(core), stats, constants, own, sibling, z, cotangent, cotangent_in)


def fetch_kernel(where, mine, other, mine_pair, other_pair, out, out_pair, sem):
    for flag, pair in ((1, (mine, mine_pair)), (0, (other, other_pair))):

        @pl.when(where[0] == flag)
        def _():
            copy_all(
                [
                    pltpu.make_async_copy(x, o, sem.at[i])
                    for i, (x, o) in enumerate(zip(pair, (out, out_pair)))
                ]
            )


def fetch(flag, mine, other, mine_pair, other_pair):
    out = shape_of(mine.shape, mine.dtype)
    return call(
        fetch_kernel,
        (out, out),
        "fetch",
        in_specs=[SMEM] + [HBM] * 4,
        out_specs=(VMEM, VMEM),
        scratch_shapes=[pltpu.SemaphoreType.DMA((2,))],
    )(scalars(flag), mine, other, mine_pair, other_pair)


def weight_part_kernel(columns, agg, agg_pair, dz, dz_pair, out):
    out[...] = (
        by_rows(agg[:, columns], dz[...]) + by_rows(agg_pair[:, columns], dz_pair[...])
    ).astype(BF)


def weight_part(agg, agg_pair, dz, dz_pair, t):
    tall = agg.shape[1] // TILES
    return call(
        functools.partial(weight_part_kernel, slice(t * tall, (t + 1) * tall)),
        shape_of((tall, dz.shape[1]), BF),
        "weight_part",
    )(agg, agg_pair, dz, dz_pair)


def fold_kernel(where, own, received, away, keep):
    rows = keep.shape[0]
    for side, out in ((1 - where[0], away), (where[0], keep)):
        part = pl.ds(pl.multiple_of(side * rows, rows), rows)
        out[...] = (own[part, :].astype(F32) + received[part, :].astype(F32)).astype(BF)


def fold(own, received, v, cost=FREE):
    rows, w = own.shape
    out = shape_of((rows // 2, w), BF)
    return call(fold_kernel, (out, out), "fold", in_specs=[SMEM, VMEM, VMEM], cost=cost)(
        scalars(v), own, received
    )


def total_kernel(own, received, out):
    out[...] = (own[...].astype(F32) + received[...].astype(F32)).astype(BF)


def total_of(own, received, cost=FREE):
    return call(total_kernel, shape_of(own.shape, BF), "total", cost=cost)(own, received)


def join_kernel(where, own, received, out):
    rows = own.shape[0]
    for side, x in ((where[0], own), (1 - where[0], received)):
        out[pl.ds(pl.multiple_of(side * rows, rows), rows), :] = x[...]


def join(own, received, v, cost=FREE):
    rows, w = own.shape
    return call(
        join_kernel,
        shape_of((2 * rows, w), BF),
        "join",
        in_specs=[SMEM, VMEM, VMEM],
        cost=cost,
    )(scalars(v), own, received)


def place_kernel(n, where, *refs):
    pieces, (out, wide, put) = refs[:n], refs[-3:]

    def write(i, k):
        rows, w = pieces[i].shape
        row = pl.multiple_of(where[3 * i + k], 64)
        column = pl.multiple_of(where[3 * i + 2], 128)
        return pltpu.make_async_copy(
            wide.at[i, k * (rows // 2) : (k + 1) * (rows // 2), :],
            out.at[pl.ds(row, rows // 2), pl.ds(column, w)],
            put.at[i, k],
        )

    for i in range(n):
        step = 128
        half = pieces[i].shape[0] // 2
        for k in range(2):

            @pl.loop(0, half // step)
            def _(j):
                part = pl.ds(pl.multiple_of(k * half + j * step, step), step)
                wide[i, part, :] = pieces[i][part, :].astype(F32)

            write(i, k).start()
    for i in range(n):
        for k in range(2):
            write(i, k).wait()


def place(total, pieces, shape):
    n = len(pieces)
    rows, w = pieces[0][0].shape
    operands = [scalars(*[x for p in pieces for x in p[1:]])] + [p[0] for p in pieces]
    specs = [SMEM] + [VMEM] * n
    aliases = {}
    if total is not None:
        aliases = {len(operands): 0}
        operands.append(total)
        specs.append(HBM)
    return call(
        functools.partial(place_kernel, n),
        far_shape(shape, F32),
        "place",
        in_specs=specs,
        out_specs=HBM,
        scratch_shapes=[pltpu.VMEM((n, rows, w), F32), pltpu.SemaphoreType.DMA((n, 2))],
        input_output_aliases=aliases,
    )(*operands)


def back_part_kernel(columns, where, own, sibling, dz, out):
    nodes = own.shape[0]
    total = 0.0
    for side, count in ((where[0], own), (1 - where[0], sibling)):
        rows = pl.ds(pl.multiple_of(side * nodes, nodes), nodes)
        total = total + by_rows(count[:, columns], dz[rows, :])
    out[...] = total.astype(BF)


def back_part(core, own, sibling, dz, k, parts):
    rows = own.shape[1] // parts
    return call(
        functools.partial(back_part_kernel, slice(k * rows, (k + 1) * rows)),
        shape_of((rows, dz.shape[1]), BF),
        "back_part",
        in_specs=[SMEM] + [VMEM] * 3,
    )(scalars(core), own, sibling, dz)


def halve_kernel(own, received, away, keep):
    rows = keep.shape[0]
    keep[...] = (own[:rows].astype(F32) + received[:rows].astype(F32)).astype(BF)
    away[...] = (own[rows:].astype(F32) + received[rows:].astype(F32)).astype(BF)


def halve(own, received):
    rows, w = own.shape
    out = shape_of((rows // 2, w), BF)
    return call(halve_kernel, (out, out), "halve")(own, received)


def own_back_kernel(where, own, sibling, dz, keep, away):
    nodes = keep.shape[0]
    core = where[0]
    for side, count, out in ((core, own, keep), (1 - core, sibling, away)):
        part = pl.ds(pl.multiple_of(side * nodes, nodes), nodes)
        out[...] = by_rows(count[...], dz[part, :]).astype(BF)


def own_back(core, own, sibling, dz):
    rows, half = dz.shape
    out = shape_of((rows // 2, half), BF)
    return call(own_back_kernel, (out, out), "own_back", in_specs=[SMEM] + [VMEM] * 3)(
        scalars(core), own, sibling, dz
    )


def finish_kernel(
    where, rows, back, back_in, vec, vec_in, own, own_in, act, act_in, weight,
    grad, activations, vectors, near_weight, near_own, table, weight_sem, own_sem, act_sem,
):
    core = where[0]
    nodes, half = own.shape
    sends = rows.shape[0]
    block = 512
    blocks = weight.shape[0] // block

    def side_of(k):
        return pl.ds(pl.multiple_of((core if k == 0 else 1 - core) * half, half), half)

    owns = [
        pltpu.make_async_copy(x, near_own.at[k], own_sem.at[k]) for k, x in enumerate((own, own_in))
    ]
    acts = [
        pltpu.make_async_copy(x, activations.at[:, side_of(k)], act_sem.at[k])
        for k, x in enumerate((act, act_in))
    ]
    weights = [
        pltpu.make_async_copy(
            weight.at[k * block : (k + 1) * block, :],
            near_weight.at[k * block : (k + 1) * block, :],
            weight_sem.at[k],
        )
        for k in range(blocks)
    ]
    for c in owns + weights + acts:
        c.start()
    hot = (rows[...] == lax.broadcasted_iota(jnp.int32, (sends, nodes), 1)).astype(BF)
    for k, (back_part, vector) in enumerate(((back[:sends], vec), (back_in[...], vec_in))):
        vectors[:, side_of(k)] = vector[...]
        owns[k].wait()
        part = near_own[k].astype(F32) + by_rows(hot, back_part)
        table[:, side_of(k)] = part.astype(BF)
    for k in range(blocks):
        weights[k].wait()
        part = slice(k * block, (k + 1) * block)
        grad[:, part] = lax.dot_general(
            table[...], near_weight[part, :], (((1,), (1,)), ((), ())), preferred_element_type=F32
        ).astype(BF)
    for c in acts:
        c.wait()


def finish(core, rows, back, back_in, own, own_in, act, act_in, vec, vec_in, weight):
    nodes, half = own.shape
    width = 2 * half
    return call(
        finish_kernel,
        (
            shape_of((nodes, width), BF),
            shape_of((nodes, width), BF),
            shape_of((8, width), F32),
        ),
        "finish",
        in_specs=[SMEM] + [VMEM] * 5 + [HBM] * 5,
        out_specs=(VMEM, VMEM, VMEM),
        scratch_shapes=[
            pltpu.VMEM(weight.shape, BF),
            pltpu.VMEM((2, nodes, half), BF),
            pltpu.VMEM((nodes, width), BF),
            pltpu.SemaphoreType.DMA((width // 512,)),
            pltpu.SemaphoreType.DMA((2,)),
            pltpu.SemaphoreType.DMA((2,)),
        ],
    )(scalars(core), rows, back, back_in, vec, vec_in, own, own_in, act, act_in, weight)


def on_device(
    size,
    features,
    weight,
    bias,
    gamma,
    beta,
    neighbours,
    edge_mask,
    node_mask,
    send_rows,
    send_mask,
    cotangent,
):
    nodes, width = features.shape
    sends = send_rows.shape[0]
    half = width // 2
    quarter = width // 4
    levels = size.bit_length() - 5

    me = lax.axis_index("dom")
    core = me & 1
    is0 = core == 0
    bits = {"f": (1, 2), "p": (2, 3), "q": (3, 1), "s": (2, 1), "z": (3, 3)}
    others = list(range(4, levels + 4))
    for b in others:
        bits[b] = (b, b)
    axes = ["f", "p", "q"] + others

    def bit_of(b):
        return (me >> b) & 1

    def bit(b):
        return jnp.where(is0, bit_of(bits[b][0]), bit_of(bits[b][1]))

    def weight_of(b):
        return jnp.where(is0, 1 << bits[b][0], 1 << bits[b][1])

    def peer(i, b):
        return i ^ (1 << bits[b][i & 1])

    first, sibling_first = bit("f"), jnp.where(is0, bit_of(2), bit_of(1))
    high, sibling_high = bit("p"), jnp.where(is0, bit_of(3), bit_of(2))

    def along(x, b):
        return lax.ppermute(x, "dom", [(i, peer(i, b)) for i in range(size)])

    def swap(x):
        return lax.ppermute(x, "dom", [(i, i ^ 1) for i in range(size)])

    token = [jnp.zeros((8, 128), F32)]

    def arrive(*x):
        *x, token[0] = lax.optimization_barrier((*x, token[0]))
        return x[0] if len(x) == 1 else x

    def tick():
        token[0] = tick_of(token[0])

    def start(generators):
        running = dict(generators)
        for k in running:
            next(running[k])
        done = {}

        def advance(k):
            try:
                next(running[k])
            except StopIteration as stop:
                done[k] = stop.value

        return advance, done

    live_row = jnp.where(send_mask > 0, send_rows, -1)[:, None]
    out_away, *out_keep = outgoing_rows(
        core, live_row, features, HALO_WIDTHS
    )
    outgoing = stack(out_keep, arrive(swap(out_away)))
    halo_rows = sends * size
    chip_rows = 2 * sends

    def gather_halo(k, x):
        for b in reversed(axes):
            received = along(x, b)
            yield
            x = stack_rows(x, arrive(received), SMALL if k else FREE)
        return x

    generators = {k: gather_halo(k, x) for k, x in enumerate(outgoing)}
    advance, halo = start(generators)

    def hop():
        for k in generators:
            advance(k)

    live_neighbour = jnp.where(edge_mask > 0, neighbours, -1)
    packed = jnp.concatenate([live_neighbour, node_mask[:, None]], 1)
    place_of = jnp.arange(halo_rows)
    chip, row = place_of // chip_rows, place_of % chip_rows
    relative = 0
    for k, b in enumerate(axes):
        relative = relative + ((chip >> (len(axes) - 1 - k)) & 1) * weight_of(b)
    owner = (me ^ relative) ^ (row // sends)
    label = (nodes + owner * sends + row % sends)[None, :]
    packed, label = arrive(packed, label)
    sibling_packed = arrive(swap(packed))
    hop()
    features_in, cotangent_in = swap(features), swap(cotangent)
    constants = jnp.stack([bias, gamma, beta])
    packed = arrive(packed)
    own = arrive(*counts(packed, label))
    constants = arrive(constants)
    hop()
    features_in, cotangent_in, sibling_packed = arrive(features_in, cotangent_in, sibling_packed)
    sibling = arrive(*counts(sibling_packed, label))
    hop()
    for _ in range(levels):
        hop()

    agg_mine = aggregate(
        core, features, features_in, own, sibling, [halo[k] for k in generators]
    )
    agg_other = swap(agg_mine)
    mine_pair = along(agg_mine, "f")
    agg_other = arrive(agg_other)
    other_pair = along(agg_other, "f")
    z, stats = forward(
        core, agg_mine, agg_other, weight, constants, cotangent, cotangent_in, own[2], sibling[2]
    )

    same = (high == core).astype(jnp.int32)
    for k, b in enumerate(others + ["q", "p", "f"]):
        received = along(stats, b)
        if k == 0:
            mine_pair = arrive(mine_pair)
        if b == "f":
            other_pair = arrive(other_pair)
        stats = merge(stats, arrive(received), bit(b))
    nodes_args = (z, stats, constants, cotangent, cotangent_in, own[2], sibling[2])
    dz_send = dz_of(core, 1 - first, *nodes_args)

    dz_pair = along(dz_send, "f")
    aggs = (agg_mine, agg_other, mine_pair, other_pair)
    dz_send = arrive(dz_send)
    dz_keep = dz_of(core, first, *nodes_args)
    away = fetch(1 - same, *aggs)
    dz_keep, *away = arrive(dz_keep, *away)
    dz_pair = arrive(dz_pair)

    def weight_gradient(t):
        cost = SMALL if t else FREE
        received = along(weight_part(*away, dz_keep, dz_pair, t), "p")
        yield
        part = weight_part(*keep, dz_keep, dz_pair, t)
        part = arrive(part)
        yield
        received = arrive(received)
        for b in axes[2:]:
            out, part = fold(part, received, bit(b), cost)
            received = along(out, b)
            yield
            received = arrive(received)
        part = total_of(part, received, cost)
        for b in others[::-1] + [LAST[0]]:
            received = along(part, b)
            yield
            part = join(part, arrive(received), bit(b), cost)
        return part

    def reduce_halo():
        received, part = along(back_send, axes[0]), back_keep
        for b in axes[1:]:
            yield
            out, part = halve(part, arrive(received))
            received = along(out, b)
        yield
        return total_of(part, arrive(received))

    generators = {"d%d" % t: weight_gradient(t) for t in range(TILES)}
    advance, found = start(generators)
    groups = {k: [1, 1, len(others), len(others), 1] for k in generators}
    groups["h"] = [1, 1, 1, len(others)]
    tall = half // TILES
    tiles = range(TILES)
    shape = (width, width)
    if LAST[1] == "z":
        layers = bit_of(3), bit_of(3)
        steps = jnp.where(is0, half, tall // 2), jnp.where(is0, tall // 2, half)
        steps = steps, steps[::-1]
    else:
        layers = high, sibling_high
        steps = ((tall // 2, half),) * 2

    def pieces(own, sibling, away, other):
        placed = []
        for side, arrays in enumerate((own, sibling)):
            begin = core if side == 0 else 1 - core
            f = first if side == 0 else sibling_first
            inner, outer = steps[side]
            z = 1 - layers[side] if away else layers[side]
            for t, x in enumerate(arrays):
                row = t * tall + z * outer
                column = begin * half + (1 - f if other else f) * quarter
                placed.append((x, row, row + inner, column))
        return placed

    across, pair, here = [None] * TILES, [None] * TILES, [None] * TILES
    here_across, here_pair, pair_across = [None] * TILES, [None] * TILES, [None] * TILES
    for action in ORDER.split():
        if action == "K":
            keep = arrive(*fetch(same, *aggs))
            for k in generators:
                advance(k)
        elif action == "O":
            dz_scaled, act, act_away, vectors = arrive(*outputs(core, *nodes_args))
        elif action == "G":
            dz_scaled = arrive(dz_scaled)
            back_send, back_keep = arrive(
                *(back_part(core, own[0], sibling[0], dz_scaled, k, 2) for k in (1, 0))
            )
        elif action == "H":
            back_send = arrive(back_send)
            advance_halo, halo_part = start({"h": reduce_halo()})
        elif action == "B":
            dz_scaled = arrive(dz_scaled)
            kept_back, away_back = arrive(*own_back(core, own[1], sibling[1], dz_scaled))
            own_in, act_in, vectors_in = swap(away_back), swap(act_away), swap(vectors)
        elif action == "b":
            own_in, act_in, vectors_in = arrive(own_in, act_in, vectors_in)
        elif action == "t":
            tick()
        elif action in groups:
            step = advance_halo if action == "h" else advance
            for _ in range(groups[action].pop(0)):
                step(action)
            if action in found:
                t = list(generators).index(action)
                across[t], pair[t] = along(found[action], LAST[1]), along(found[action], "f")
                here[t] = swap(found[action])
        elif action == "e":
            here = [arrive(x) for x in here]
            part = [found[k] for k in generators]
            total = arrive(place(None, pieces(part, here, False, False), shape))
        elif action[0] == "x":
            t = int(action[1])
            across[t] = arrive(across[t])
            here_across[t], pair_across[t] = swap(across[t]), along(across[t], "f")
        elif action[0] == "p":
            t = int(action[1])
            pair[t] = arrive(pair[t])
            here_pair[t] = swap(pair[t])
        elif action == "R":
            back = halo_part["h"]
            back_in = arrive(swap(back[sends:]))
        elif action == "F":
            grad_features, activations, vectors = arrive(
                *finish(
                    core, live_row, back, back_in, kept_back, own_in, act, act_in, vectors, vectors_in, weight
                )
            )
        elif action == "P":
            here_across = [arrive(x) for x in here_across]
            here_pair = [arrive(x) for x in here_pair]
            total = place(
                total,
                pieces(across, here_across, True, False) + pieces(pair, here_pair, False, True),
                shape,
            )
            total = arrive(total)
    pair_across = [arrive(x) for x in pair_across]
    vectors = vectors + token[0][0, 0]
    here_pair_across = [swap(x) for x in pair_across]
    total = place(total, pieces(pair_across, here_pair_across, True, True), shape)
    return activations, grad_features, total, vectors[0], vectors[1], vectors[2]


def solution(mesh):
    size = mesh.shape["dom"]
    return jax.shard_map(
        functools.partial(on_device, size),
        mesh=mesh,
        in_specs=(
            P("dom", None),
            P(),
            P(),
            P(),
            P(),
            P("dom", None),
            P("dom", None),
            P("dom"),
            P("dom"),
            P("dom"),
            P("dom", None),
        ),
        out_specs=(P("dom", None), P("dom", None), P(), P(), P(), P()),
        check_vma=False,
    )
```

```python
import functools

import jax
import jax.numpy as jnp
from jax import lax
from jax.experimental import pallas as pl
from jax.experimental.pallas import tpu as pltpu
from jax.sharding import PartitionSpec as P

BF = jnp.bfloat16
F32 = jnp.float32
MIB = 1 << 20
HALO_WIDTHS = (512, 512)
TILES = 2
LAST = ("q", "p")
ORDER = (
    "K", "O", "d0", "d1", "G", "d0", "d1", "H", "B", "d0", "d1", "t", "h", "d0", "d1", "b", "t",
    "h", "d0", "d1", "t", "h", "e", "x0", "t", "p0", "h", "x1", "p1", "t", "R", "t", "F", "P",
)

FREE = pl.CostEstimate(flops=0, bytes_accessed=0, transcendentals=0)
LARGE = pl.CostEstimate(flops=5_000_000_000, bytes_accessed=0, transcendentals=0)
HBM = pl.BlockSpec(memory_space=pltpu.HBM)
SMEM = pl.BlockSpec(memory_space=pltpu.SMEM)
VMEM = pl.BlockSpec(memory_space=pltpu.VMEM)
BY_ROWS = (((0,), (0,)), ((), ()))


def shape_of(shape, dtype):
    return jax.ShapeDtypeStruct(shape, dtype)


def far_shape(shape, dtype):
    return pltpu.HBM(shape, dtype)


def call(body, out_shape, name, vmem=24, cost=FREE, **rest):
    kernel = pl.pallas_call(
        body,
        out_shape=out_shape,
        compiler_params=pltpu.CompilerParams(vmem_limit_bytes=vmem * MIB),
        cost_estimate=cost,
        name=name,
        **rest,
    )
    specs = rest.get("in_specs")

    def run(*operands):
        if specs is None:
            return kernel(*operands)
        return kernel(
            *[
                pltpu.with_memory_space_constraint(x, pltpu.HBM) if spec is HBM else x
                for x, spec in zip(operands, specs)
            ]
        )

    return run


def scalars(*x):
    return jnp.stack([jnp.int32(v) for v in x])


def mxu(a, b):
    return jnp.dot(a, b, preferred_element_type=F32)


def by_rows(a, b):
    return lax.dot_general(a, b, BY_ROWS, preferred_element_type=F32)


def copy_all(copies):
    for c in copies:
        c.start()
    for c in copies:
        c.wait()


def tick_kernel(x, out):
    out[...] = x[...]


def tick_of(x):
    return call(tick_kernel, shape_of(x.shape, x.dtype), "tick", cost=LARGE)(x)


def outgoing_kernel(where, rows, features, away, *keep):
    nodes, width = features.shape
    half = width // 2
    hot = (rows[...] == lax.broadcasted_iota(jnp.int32, (rows.shape[0], nodes), 1)).astype(BF)
    there = features[:, pl.ds(pl.multiple_of((1 - where[0]) * half, half), half)]
    away[...] = mxu(hot, there).astype(BF)
    here = mxu(hot, features[:, pl.ds(pl.multiple_of(where[0] * half, half), half)]).astype(BF)
    at = 0
    for out in keep:
        out[...] = here[:, at : at + out.shape[1]]
        at += out.shape[1]


def outgoing_rows(core, rows, features, widths):
    sends, half = rows.shape[0], features.shape[1] // 2
    return call(
        outgoing_kernel,
        tuple(shape_of((sends, w), BF) for w in (half,) + widths),
        "outgoing",
        in_specs=[SMEM, VMEM, VMEM],
    )(scalars(core), rows, features)


def stack_kernel(n, received, *refs):
    own, outs = refs[:n], refs[n:]
    at = 0
    for x, out in zip(own, outs):
        rows, w = x.shape
        out[:rows, :] = x[...]
        out[rows:, :] = received[:, at : at + w]
        at += w


def stack(own, received):
    return call(
        functools.partial(stack_kernel, len(own)),
        tuple(shape_of((2 * x.shape[0], x.shape[1]), BF) for x in own),
        "stack",
    )(received, *own)


def stack_rows_kernel(own, received, out):
    rows = own.shape[0]
    out[:rows, :] = own[...]
    out[rows:, :] = received[...]


def stack_rows(own, received):
    rows, w = own.shape
    return call(stack_rows_kernel, shape_of((2 * rows, w), own.dtype), "stack_rows")(
        own, received
    )


def counts_kernel(packed, label, halo_count, own_count, factors):
    nodes, columns = packed.shape
    slots = columns - 1

    def count(labels):
        total = jnp.zeros((nodes, labels.shape[1]), F32)
        for e in range(slots):
            total = total + jnp.where(packed[:, e : e + 1] == labels, 1.0, 0.0)
        return total

    halo_count[...] = count(label[...]).astype(BF)
    local = lax.broadcasted_iota(jnp.int32, (nodes, nodes), 1)
    row = lax.broadcasted_iota(jnp.int32, (nodes, nodes), 0)
    own_count[...] = (count(local) + jnp.where(row == local, 2.0, 0.0)).astype(BF)
    degree = jnp.zeros((nodes, 1), F32)
    for e in range(slots):
        degree = degree + jnp.where(packed[:, e : e + 1] >= 0, 1.0, 0.0)
    lane = lax.broadcasted_iota(jnp.int32, factors.shape, 1)
    factors[...] = jnp.where(lane == 0, packed[:, slots:].astype(F32), 1.0 / (degree + 1.0))


def counts(packed, label):
    nodes = packed.shape[0]
    return call(
        counts_kernel,
        (
            shape_of((nodes, label.shape[1]), BF),
            shape_of((nodes, nodes), BF),
            shape_of((nodes, 128), F32),
        ),
        "counts",
    )(packed, label)


def aggregate_kernel(n, where, features, features_in, *refs):
    own, sibling, halos = refs[:3], refs[3:6], refs[6 : 6 + n]
    out, near, sem = refs[6 + n :]
    _, nodes, half = near.shape
    core = where[0]
    here = pl.ds(pl.multiple_of(core * half, half), half)
    copies = [
        pltpu.make_async_copy(x.at[:, here], near.at[k], sem.at[k])
        for k, x in enumerate((features, features_in))
    ]
    for c in copies:
        c.start()
    for k, (halo_count, own_count, factors) in enumerate((own, sibling)):
        rows = pl.ds(pl.multiple_of((core if k == 0 else 1 - core) * nodes, nodes), nodes)
        start = 0
        for i, halo in enumerate(halos):
            part = slice(start, start + halo.shape[1])
            total = mxu(halo_count[...], halo[...])
            if i == 0:
                copies[k].wait()
            total = total + mxu(own_count[...], near[k][:, part])
            out[rows, part] = (total * factors[:, 1:2]).astype(BF)
            start += halo.shape[1]


def aggregate(core, features, features_in, own, sibling, halos):
    rows, width = features.shape
    half = width // 2
    return call(
        functools.partial(aggregate_kernel, len(halos)),
        shape_of((2 * rows, half), BF),
        "aggregate",
        in_specs=[SMEM, HBM, HBM] + [VMEM] * (6 + len(halos)),
        scratch_shapes=[pltpu.VMEM((2, rows, half), BF), pltpu.SemaphoreType.DMA((2,))],
    )(scalars(core), features, features_in, *own, *sibling, *halos)


def grad_loads(core, cotangent, cotangent_in, near_g, column, sems):
    rows, width = cotangent.shape
    start, size = column
    whole = pl.ds(pl.multiple_of(core * (width // 2) + start, 256), size)
    own = pl.ds(pl.multiple_of(core * rows, rows), rows)
    far = pl.ds(pl.multiple_of((1 - core) * rows, rows), rows)
    return [
        pltpu.make_async_copy(cotangent.at[:, whole], near_g.at[own, :], sems.at[0]),
        pltpu.make_async_copy(cotangent_in.at[:, whole], near_g.at[far, :], sems.at[1]),
    ]


def factor(core, own, other, lane):
    return jnp.concatenate(
        [jnp.where(core == k, own[:, lane : lane + 1], other[:, lane : lane + 1]) for k in range(2)], 0
    )


def forward_kernel(
    where, mine, other, constants, own_factors, other_factors,
    weight, cotangent, cotangent_in,
    z_out, stats_ref, near_mine, near_other, near_g, z_ref, sem, out_sem,
):
    core = where[0]
    block = 256
    half = z_ref.shape[1]
    own = pl.ds(pl.multiple_of(core * half, half), half)
    far = pl.ds(pl.multiple_of((1 - core) * half, half), half)

    def loads(k, start, size):
        whole = pl.ds(pl.multiple_of(core * half + start, 256), size)
        part = slice(start, start + size)
        return [
            pltpu.make_async_copy(weight.at[own, whole], near_mine.at[:, part], sem.at[0, k]),
            pltpu.make_async_copy(weight.at[far, whole], near_other.at[:, part], sem.at[1, k]),
        ]

    ranges = ((0, block), (block, half - block))
    copies = [loads(k, *r) for k, r in enumerate(ranges)]
    grads = grad_loads(core, cotangent, cotangent_in, near_g, (0, half), sem.at[2])
    for c in copies[0] + grads + copies[1]:
        c.start()

    def store(j):
        part = slice(2 * j * block, 2 * (j + 1) * block)
        return pltpu.make_async_copy(z_ref.at[:, part], z_out.at[:, part], out_sem.at[j])

    valid = factor(core, own_factors, other_factors, 0)
    bias = constants[0:1, own]
    for j in range(half // block):
        at = slice(j * block, (j + 1) * block)
        if j < 2:
            for c in copies[j]:
                c.wait()
        z_ref[:, at] = (
            mxu(mine[...], near_mine[:, at]) + mxu(other[...], near_other[:, at]) + bias[:, at]
        )
        if j == 0:
            for c in grads:
                c.wait()
        if j % 2 == 1:
            store(j // 2).start()
        z = z_ref[:, at]
        sigma = 1.0 / (1.0 + jnp.exp(-z))
        y = z * sigma
        slope = (sigma + y * (1.0 - sigma)) * valid
        g = near_g[:, at].astype(F32) * valid

        def column(x):
            return jnp.sum(x, axis=0, keepdims=True)

        count = jnp.broadcast_to(column(valid), (1, block))
        y_sum = column(y * valid)
        centred = (y - y_sum / jnp.maximum(count, 1.0)) * valid
        stats_ref[0:1, at] = count
        stats_ref[1:2, at] = y_sum
        stats_ref[2:3, at] = column(centred * centred)
        stats_ref[3:4, at] = column(g)
        stats_ref[4:5, at] = column(g * centred)
        stats_ref[5:6, at] = column(slope * g)
        stats_ref[6:7, at] = column(slope)
        stats_ref[7:8, at] = column(slope * centred)
    for j in range(half // block // 2):
        store(j).wait()


def forward(core, mine, other, weight, constants, cotangent, cotangent_in, own, sibling):
    rows, half = cotangent.shape[0], mine.shape[1]
    return call(
        forward_kernel,
        (far_shape((2 * rows, half), F32), shape_of((8, half), F32)),
        "forward",
        in_specs=[SMEM] + [VMEM] * 5 + [HBM] * 3,
        out_specs=(HBM, VMEM),
        scratch_shapes=[
            pltpu.VMEM((half, half), BF),
            pltpu.VMEM((half, half), BF),
            pltpu.VMEM((2 * rows, half), BF),
            pltpu.VMEM((2 * rows, half), F32),
            pltpu.SemaphoreType.DMA((3, 2)),
            pltpu.SemaphoreType.DMA((half // 512,)),
        ],
    )(
        scalars(core), mine, other, constants, own, sibling, weight, cotangent, cotangent_in
    )


def merge_kernel(where, own, received, out):
    upper = where[0] == 1
    a, b = own[...], received[...]
    a, b = jnp.where(upper, b, a), jnp.where(upper, a, b)

    def row(x, k):
        return x[k : k + 1, :]

    na, nb = row(a, 0), row(b, 0)
    n = na + nb
    mean = (row(a, 1) + row(b, 1)) / jnp.maximum(n, 1.0)
    da = row(a, 1) / jnp.maximum(na, 1.0) - mean
    db = row(b, 1) / jnp.maximum(nb, 1.0) - mean
    out[...] = a + b
    out[2:3, :] = (row(a, 2) + na * da * da) + (row(b, 2) + nb * db * db)
    out[4:5, :] = (row(a, 4) + da * row(a, 3)) + (row(b, 4) + db * row(b, 3))
    out[7:8, :] = (row(a, 7) + da * row(a, 6)) + (row(b, 7) + db * row(b, 6))


def merge(own, received, v):
    return call(
        merge_kernel, shape_of(own.shape, F32), "merge", in_specs=[SMEM, VMEM, VMEM]
    )(scalars(v), own, received)


def gradient(where, at, stats_ref, constants, z, g_in, valid):
    core, half, start = where
    size = z.shape[1]
    vector = pl.ds(pl.multiple_of(core * half + start, size), size)
    stats = stats_ref[:, at]
    gamma, beta = constants[1:2, vector], constants[2:3, vector]
    n = stats[0:1, :]
    mean = stats[1:2, :] / n
    deviation = lax.rsqrt(stats[2:3, :] / n + 1e-05)
    shift = stats[3:4, :]
    scale = deviation * stats[4:5, :]
    gain = gamma * deviation
    vectors = (
        gain * (stats[5:6, :] - shift / n * stats[6:7, :] - deviation * scale / n * stats[7:8, :]),
        scale,
        shift,
    )
    sigma = 1.0 / (1.0 + jnp.exp(-z))
    y = z * sigma
    slope = (sigma + y * (1.0 - sigma)) * valid
    g = g_in.astype(F32) * valid
    normalized = (y - mean) * deviation
    dz = gain * (g - shift / n - normalized * (scale / n)) * slope
    return dz, valid * (gamma * normalized + beta), vectors


def dz_kernel(
    where, stats_ref, constants, own_factors, other_factors, z_ref, cotangent, cotangent_in,
    out, near_z, near_g, sem,
):
    side, core = where[0], where[1]
    half, size = z_ref.shape[1], out.shape[1]
    block = 256
    blocks = size // block

    def loads(k):
        start = side * size + k * block
        part = pl.ds(pl.multiple_of(start, block), block)
        here = slice(k * block, (k + 1) * block)
        copy = pltpu.make_async_copy(z_ref.at[:, part], near_z.at[:, here], sem.at[k, 2])
        return [copy] + grad_loads(
            core, cotangent, cotangent_in, near_g.at[:, here], (start, block), sem.at[k]
        )

    copies = [loads(k) for k in range(blocks)]
    for c in copies[0] + copies[1]:
        c.start()
    valid = factor(core, own_factors, other_factors, 0)
    for k in range(blocks):
        for c in copies[k]:
            c.wait()
        here = slice(k * block, (k + 1) * block)
        start = side * size + k * block
        at = pl.ds(pl.multiple_of(start, block), block)
        dz, _, _ = gradient(
            (core, half, start), at, stats_ref, constants, near_z[:, here], near_g[:, here], valid
        )
        out[:, here] = dz.astype(BF)


def dz_of(core, side, z, stats, constants, cotangent, cotangent_in, own, sibling):
    rows, half = z.shape
    return call(
        dz_kernel,
        shape_of((rows, half // 2), BF),
        "dz",
        in_specs=[SMEM] + [VMEM] * 4 + [HBM] * 3,
        scratch_shapes=[
            pltpu.VMEM((rows, half // 2), F32),
            pltpu.VMEM((rows, half // 2), BF),
            pltpu.SemaphoreType.DMA((2, 3)),
        ],
    )(scalars(side, core), stats, constants, own, sibling, z, cotangent, cotangent_in)


def outputs_kernel(
    where, stats_ref, constants, own_factors, other_factors, z_ref, cotangent, cotangent_in,
    dz_scaled, act_keep, act_away, vectors, near_z, near_g, sem,
):
    core = where[0]
    rows, half = z_ref.shape
    nodes = rows // 2
    block = 256
    copies = [pltpu.make_async_copy(z_ref, near_z, sem.at[2])]
    copies += grad_loads(core, cotangent, cotangent_in, near_g, (0, half), sem)
    for c in copies:
        c.start()
    valid, inverse = (factor(core, own_factors, other_factors, lane) for lane in range(2))
    for c in copies:
        c.wait()
    vectors[3:8, :] = jnp.zeros((5, half), F32)
    for k in range(half // block):
        at = slice(k * block, (k + 1) * block)
        dz, act, sums = gradient(
            (core, half, k * block), at, stats_ref, constants, near_z[:, at], near_g[:, at], valid
        )
        dz_scaled[:, at] = (dz * inverse).astype(BF)
        act = act.astype(BF)
        act_keep[:, at] = jnp.where(core == 0, act[:nodes], act[nodes:])
        act_away[:, at] = jnp.where(core == 0, act[nodes:], act[:nodes])
        for i, x in enumerate(sums):
            vectors[i : i + 1, at] = x


def outputs(core, z, stats, constants, cotangent, cotangent_in, own, sibling):
    rows, half = z.shape
    act = shape_of((rows // 2, half), BF)
    return call(
        outputs_kernel,
        (shape_of((rows, half), BF), act, act, shape_of((8, half), F32)),
        "outputs",
        in_specs=[SMEM] + [VMEM] * 4 + [HBM] * 3,
        scratch_shapes=[
            pltpu.VMEM((rows, half), F32),
            pltpu.VMEM((rows, half), BF),
            pltpu.SemaphoreType.DMA((3,)),
        ],
    )(scalars(core), stats, constants, own, sibling, z, cotangent, cotangent_in)


def fetch_kernel(where, mine, other, mine_pair, other_pair, out, out_pair, sem):
    for flag, pair in ((1, (mine, mine_pair)), (0, (other, other_pair))):

        @pl.when(where[0] == flag)
        def _():
            copy_all(
                [
                    pltpu.make_async_copy(x, o, sem.at[i])
                    for i, (x, o) in enumerate(zip(pair, (out, out_pair)))
                ]
            )


def fetch(flag, mine, other, mine_pair, other_pair):
    out = shape_of(mine.shape, mine.dtype)
    return call(
        fetch_kernel,
        (out, out),
        "fetch",
        in_specs=[SMEM] + [HBM] * 4,
        out_specs=(VMEM, VMEM),
        scratch_shapes=[pltpu.SemaphoreType.DMA((2,))],
    )(scalars(flag), mine, other, mine_pair, other_pair)


def weight_part_kernel(columns, agg, agg_pair, dz, dz_pair, out):
    out[...] = (
        by_rows(agg[:, columns], dz[...]) + by_rows(agg_pair[:, columns], dz_pair[...])
    ).astype(BF)


def weight_part(agg, agg_pair, dz, dz_pair, t):
    tall = agg.shape[1] // TILES
    return call(
        functools.partial(weight_part_kernel, slice(t * tall, (t + 1) * tall)),
        shape_of((tall, dz.shape[1]), BF),
        "weight_part",
    )(agg, agg_pair, dz, dz_pair)


def fold_kernel(where, own, received, away, keep):
    rows = keep.shape[0]
    for side, out in ((1 - where[0], away), (where[0], keep)):
        part = pl.ds(pl.multiple_of(side * rows, rows), rows)
        out[...] = (own[part, :].astype(F32) + received[part, :].astype(F32)).astype(BF)


def fold(own, received, v):
    rows, w = own.shape
    out = shape_of((rows // 2, w), BF)
    return call(fold_kernel, (out, out), "fold", in_specs=[SMEM, VMEM, VMEM])(
        scalars(v), own, received
    )


def total_kernel(own, received, out):
    out[...] = (own[...].astype(F32) + received[...].astype(F32)).astype(BF)


def total_of(own, received):
    return call(total_kernel, shape_of(own.shape, BF), "total")(own, received)


def join_kernel(where, own, received, out):
    rows = own.shape[0]
    for side, x in ((where[0], own), (1 - where[0], received)):
        out[pl.ds(pl.multiple_of(side * rows, rows), rows), :] = x[...]


def join(own, received, v):
    rows, w = own.shape
    return call(
        join_kernel,
        shape_of((2 * rows, w), BF),
        "join",
        in_specs=[SMEM, VMEM, VMEM],
    )(scalars(v), own, received)


def place_kernel(n, where, *refs):
    pieces, (out, wide, put) = refs[:n], refs[-3:]

    def write(i, k):
        rows, w = pieces[i].shape
        row = pl.multiple_of(where[3 * i + k], 64)
        column = pl.multiple_of(where[3 * i + 2], 128)
        return pltpu.make_async_copy(
            wide.at[i, k * (rows // 2) : (k + 1) * (rows // 2), :],
            out.at[pl.ds(row, rows // 2), pl.ds(column, w)],
            put.at[i, k],
        )

    for i in range(n):
        step = 128
        half = pieces[i].shape[0] // 2
        for k in range(2):

            @pl.loop(0, half // step)
            def _(j):
                part = pl.ds(pl.multiple_of(k * half + j * step, step), step)
                wide[i, part, :] = pieces[i][part, :].astype(F32)

            write(i, k).start()
    for i in range(n):
        for k in range(2):
            write(i, k).wait()


def place(total, pieces, shape):
    n = len(pieces)
    rows, w = pieces[0][0].shape
    operands = [scalars(*[x for p in pieces for x in p[1:]])] + [p[0] for p in pieces]
    specs = [SMEM] + [VMEM] * n
    aliases = {}
    if total is not None:
        aliases = {len(operands): 0}
        operands.append(total)
        specs.append(HBM)
    return call(
        functools.partial(place_kernel, n),
        far_shape(shape, F32),
        "place",
        in_specs=specs,
        out_specs=HBM,
        scratch_shapes=[pltpu.VMEM((n, rows, w), F32), pltpu.SemaphoreType.DMA((n, 2))],
        input_output_aliases=aliases,
    )(*operands)


def back_part_kernel(columns, where, own, sibling, dz, out):
    nodes = own.shape[0]
    total = 0.0
    for side, count in ((where[0], own), (1 - where[0], sibling)):
        rows = pl.ds(pl.multiple_of(side * nodes, nodes), nodes)
        total = total + by_rows(count[:, columns], dz[rows, :])
    out[...] = total.astype(BF)


def back_part(core, own, sibling, dz, k, parts):
    rows = own.shape[1] // parts
    return call(
        functools.partial(back_part_kernel, slice(k * rows, (k + 1) * rows)),
        shape_of((rows, dz.shape[1]), BF),
        "back_part",
        in_specs=[SMEM] + [VMEM] * 3,
    )(scalars(core), own, sibling, dz)


def halve_kernel(own, received, away, keep):
    rows = keep.shape[0]
    keep[...] = (own[:rows].astype(F32) + received[:rows].astype(F32)).astype(BF)
    away[...] = (own[rows:].astype(F32) + received[rows:].astype(F32)).astype(BF)


def halve(own, received):
    rows, w = own.shape
    out = shape_of((rows // 2, w), BF)
    return call(halve_kernel, (out, out), "halve")(own, received)


def own_back_kernel(where, own, sibling, dz, keep, away):
    nodes = keep.shape[0]
    core = where[0]
    for side, count, out in ((core, own, keep), (1 - core, sibling, away)):
        part = pl.ds(pl.multiple_of(side * nodes, nodes), nodes)
        out[...] = by_rows(count[...], dz[part, :]).astype(BF)


def own_back(core, own, sibling, dz):
    rows, half = dz.shape
    out = shape_of((rows // 2, half), BF)
    return call(own_back_kernel, (out, out), "own_back", in_specs=[SMEM] + [VMEM] * 3)(
        scalars(core), own, sibling, dz
    )


def finish_kernel(
    where, rows, back, back_in, vec, vec_in, own, own_in, act, act_in, weight,
    grad, activations, vectors, near_weight, near_own, table, weight_sem, own_sem, act_sem,
):
    core = where[0]
    nodes, half = own.shape
    sends = rows.shape[0]
    block = 512
    blocks = weight.shape[0] // block

    def side_of(k):
        return pl.ds(pl.multiple_of((core if k == 0 else 1 - core) * half, half), half)

    owns = [
        pltpu.make_async_copy(x, near_own.at[k], own_sem.at[k]) for k, x in enumerate((own, own_in))
    ]
    acts = [
        pltpu.make_async_copy(x, activations.at[:, side_of(k)], act_sem.at[k])
        for k, x in enumerate((act, act_in))
    ]
    weights = [
        pltpu.make_async_copy(
            weight.at[k * block : (k + 1) * block, :],
            near_weight.at[k * block : (k + 1) * block, :],
            weight_sem.at[k],
        )
        for k in range(blocks)
    ]
    for c in owns + weights + acts:
        c.start()
    hot = (rows[...] == lax.broadcasted_iota(jnp.int32, (sends, nodes), 1)).astype(BF)
    for k, (back_part, vector) in enumerate(((back[:sends], vec), (back_in[...], vec_in))):
        vectors[:, side_of(k)] = vector[...]
        owns[k].wait()
        part = near_own[k].astype(F32) + by_rows(hot, back_part)
        table[:, side_of(k)] = part.astype(BF)
    for k in range(blocks):
        weights[k].wait()
        part = slice(k * block, (k + 1) * block)
        grad[:, part] = lax.dot_general(
            table[...], near_weight[part, :], (((1,), (1,)), ((), ())), preferred_element_type=F32
        ).astype(BF)
    for c in acts:
        c.wait()


def finish(core, rows, back, back_in, own, own_in, act, act_in, vec, vec_in, weight):
    nodes, half = own.shape
    width = 2 * half
    return call(
        finish_kernel,
        (
            shape_of((nodes, width), BF),
            shape_of((nodes, width), BF),
            shape_of((8, width), F32),
        ),
        "finish",
        in_specs=[SMEM] + [VMEM] * 5 + [HBM] * 5,
        out_specs=(VMEM, VMEM, VMEM),
        scratch_shapes=[
            pltpu.VMEM(weight.shape, BF),
            pltpu.VMEM((2, nodes, half), BF),
            pltpu.VMEM((nodes, width), BF),
            pltpu.SemaphoreType.DMA((width // 512,)),
            pltpu.SemaphoreType.DMA((2,)),
            pltpu.SemaphoreType.DMA((2,)),
        ],
    )(scalars(core), rows, back, back_in, vec, vec_in, own, own_in, act, act_in, weight)


def on_device(
    size,
    features,
    weight,
    bias,
    gamma,
    beta,
    neighbours,
    edge_mask,
    node_mask,
    send_rows,
    send_mask,
    cotangent,
):
    nodes, width = features.shape
    sends = send_rows.shape[0]
    half = width // 2
    quarter = width // 4
    levels = size.bit_length() - 5

    me = lax.axis_index("dom")
    core = me & 1
    is0 = core == 0
    bits = {"f": (1, 2), "p": (2, 3), "q": (3, 1), "s": (2, 1), "z": (3, 3)}
    others = list(range(4, levels + 4))
    for b in others:
        bits[b] = (b, b)
    axes = ["f", "p", "q"] + others

    def bit_of(b):
        return (me >> b) & 1

    def bit(b):
        return jnp.where(is0, bit_of(bits[b][0]), bit_of(bits[b][1]))

    def weight_of(b):
        return jnp.where(is0, 1 << bits[b][0], 1 << bits[b][1])

    def peer(i, b):
        return i ^ (1 << bits[b][i & 1])

    first, sibling_first = bit("f"), jnp.where(is0, bit_of(2), bit_of(1))
    high, sibling_high = bit("p"), jnp.where(is0, bit_of(3), bit_of(2))

    def along(x, b):
        return lax.ppermute(x, "dom", [(i, peer(i, b)) for i in range(size)])

    def swap(x):
        return lax.ppermute(x, "dom", [(i, i ^ 1) for i in range(size)])

    token = [jnp.zeros((8, 128), F32)]

    def arrive(*x):
        *x, token[0] = lax.optimization_barrier((*x, token[0]))
        return x[0] if len(x) == 1 else x

    def tick():
        token[0] = tick_of(token[0])

    def start(generators):
        running = dict(generators)
        for k in running:
            next(running[k])
        done = {}

        def advance(k):
            try:
                next(running[k])
            except StopIteration as stop:
                done[k] = stop.value

        return advance, done

    live_row = jnp.where(send_mask > 0, send_rows, -1)[:, None]
    out_away, *out_keep = outgoing_rows(
        core, live_row, features, HALO_WIDTHS
    )
    outgoing = stack(out_keep, arrive(swap(out_away)))
    halo_rows = sends * size
    chip_rows = 2 * sends

    def gather_halo(x):
        for b in reversed(axes):
            received = along(x, b)
            yield
            x = stack_rows(x, arrive(received))
        return x

    generators = {k: gather_halo(x) for k, x in enumerate(outgoing)}
    advance, halo = start(generators)

    def hop():
        for k in generators:
            advance(k)

    live_neighbour = jnp.where(edge_mask > 0, neighbours, -1)
    packed = jnp.concatenate([live_neighbour, node_mask[:, None]], 1)
    place_of = jnp.arange(halo_rows)
    chip, row = place_of // chip_rows, place_of % chip_rows
    relative = 0
    for k, b in enumerate(axes):
        relative = relative + ((chip >> (len(axes) - 1 - k)) & 1) * weight_of(b)
    owner = (me ^ relative) ^ (row // sends)
    label = (nodes + owner * sends + row % sends)[None, :]
    packed, label = arrive(packed, label)
    sibling_packed = arrive(swap(packed))
    hop()
    features_in, cotangent_in = swap(features), swap(cotangent)
    constants = jnp.stack([bias, gamma, beta])
    packed = arrive(packed)
    own = arrive(*counts(packed, label))
    constants = arrive(constants)
    hop()
    features_in, cotangent_in, sibling_packed = arrive(features_in, cotangent_in, sibling_packed)
    sibling = arrive(*counts(sibling_packed, label))
    hop()
    for _ in range(levels):
        hop()

    agg_mine = aggregate(
        core, features, features_in, own, sibling, [halo[k] for k in generators]
    )
    agg_other = swap(agg_mine)
    mine_pair = along(agg_mine, "f")
    agg_other = arrive(agg_other)
    other_pair = along(agg_other, "f")
    z, stats = forward(
        core, agg_mine, agg_other, weight, constants, cotangent, cotangent_in, own[2], sibling[2]
    )

    same = (high == core).astype(jnp.int32)
    for k, b in enumerate(others + ["q", "p", "f"]):
        received = along(stats, b)
        if k == 0:
            mine_pair = arrive(mine_pair)
        if b == "f":
            other_pair = arrive(other_pair)
        stats = merge(stats, arrive(received), bit(b))
    nodes_args = (z, stats, constants, cotangent, cotangent_in, own[2], sibling[2])
    dz_send = dz_of(core, 1 - first, *nodes_args)

    dz_pair = along(dz_send, "f")
    aggs = (agg_mine, agg_other, mine_pair, other_pair)
    dz_send = arrive(dz_send)
    dz_keep = dz_of(core, first, *nodes_args)
    away = fetch(1 - same, *aggs)
    dz_keep, *away = arrive(dz_keep, *away)
    dz_pair = arrive(dz_pair)

    def weight_gradient(t):
        received = along(weight_part(*away, dz_keep, dz_pair, t), "p")
        yield
        part = weight_part(*keep, dz_keep, dz_pair, t)
        part = arrive(part)
        yield
        received = arrive(received)
        for b in axes[2:]:
            out, part = fold(part, received, bit(b))
            received = along(out, b)
            yield
            received = arrive(received)
        part = total_of(part, received)
        for b in others[::-1] + [LAST[0]]:
            received = along(part, b)
            yield
            part = join(part, arrive(received), bit(b))
        return part

    def reduce_halo():
        received, part = along(back_send, axes[0]), back_keep
        for b in axes[1:]:
            yield
            out, part = halve(part, arrive(received))
            received = along(out, b)
        yield
        return total_of(part, arrive(received))

    generators = {"d%d" % t: weight_gradient(t) for t in range(TILES)}
    advance, found = start(generators)
    groups = {k: [1, 1, len(others), len(others), 1] for k in generators}
    groups["h"] = [1, 1, 1, len(others)]
    tall = half // TILES
    tiles = range(TILES)
    shape = (width, width)
    if LAST[1] == "z":
        layers = bit_of(3), bit_of(3)
        steps = jnp.where(is0, half, tall // 2), jnp.where(is0, tall // 2, half)
        steps = steps, steps[::-1]
    else:
        layers = high, sibling_high
        steps = ((tall // 2, half),) * 2

    def pieces(own, sibling, away, other):
        placed = []
        for side, arrays in enumerate((own, sibling)):
            begin = core if side == 0 else 1 - core
            f = first if side == 0 else sibling_first
            inner, outer = steps[side]
            z = 1 - layers[side] if away else layers[side]
            for t, x in enumerate(arrays):
                row = t * tall + z * outer
                column = begin * half + (1 - f if other else f) * quarter
                placed.append((x, row, row + inner, column))
        return placed

    across, pair, here = [None] * TILES, [None] * TILES, [None] * TILES
    here_across, here_pair, pair_across = [None] * TILES, [None] * TILES, [None] * TILES
    for action in ORDER:
        if action == "K":
            keep = arrive(*fetch(same, *aggs))
            for k in generators:
                advance(k)
        elif action == "O":
            dz_scaled, act, act_away, vectors = arrive(*outputs(core, *nodes_args))
        elif action == "G":
            dz_scaled = arrive(dz_scaled)
            back_send, back_keep = arrive(
                *(back_part(core, own[0], sibling[0], dz_scaled, k, 2) for k in (1, 0))
            )
        elif action == "H":
            back_send = arrive(back_send)
            advance_halo, halo_part = start({"h": reduce_halo()})
        elif action == "B":
            dz_scaled = arrive(dz_scaled)
            kept_back, away_back = arrive(*own_back(core, own[1], sibling[1], dz_scaled))
            own_in, act_in, vectors_in = swap(away_back), swap(act_away), swap(vectors)
        elif action == "b":
            own_in, act_in, vectors_in = arrive(own_in, act_in, vectors_in)
        elif action == "t":
            tick()
        elif action in groups:
            step = advance_halo if action == "h" else advance
            for _ in range(groups[action].pop(0)):
                step(action)
            if action in found:
                t = list(generators).index(action)
                across[t], pair[t] = along(found[action], LAST[1]), along(found[action], "f")
                here[t] = swap(found[action])
        elif action == "e":
            here = [arrive(x) for x in here]
            part = [found[k] for k in generators]
            total = arrive(place(None, pieces(part, here, False, False), shape))
        elif action[0] == "x":
            t = int(action[1])
            across[t] = arrive(across[t])
            here_across[t], pair_across[t] = swap(across[t]), along(across[t], "f")
        elif action[0] == "p":
            t = int(action[1])
            pair[t] = arrive(pair[t])
            here_pair[t] = swap(pair[t])
        elif action == "R":
            back = halo_part["h"]
            back_in = arrive(swap(back[sends:]))
        elif action == "F":
            grad_features, activations, vectors = arrive(
                *finish(
                    core, live_row, back, back_in, kept_back, own_in, act, act_in, vectors, vectors_in, weight
                )
            )
        elif action == "P":
            here_across = [arrive(x) for x in here_across]
            here_pair = [arrive(x) for x in here_pair]
            total = place(
                total,
                pieces(across, here_across, True, False) + pieces(pair, here_pair, False, True),
                shape,
            )
            total = arrive(total)
    pair_across = [arrive(x) for x in pair_across]
    vectors = vectors + token[0][0, 0]
    here_pair_across = [swap(x) for x in pair_across]
    total = place(total, pieces(pair_across, here_pair_across, True, True), shape)
    return activations, grad_features, total, vectors[0], vectors[1], vectors[2]


def solution(mesh):
    size = mesh.shape["dom"]
    return jax.shard_map(
        functools.partial(on_device, size),
        mesh=mesh,
        in_specs=(
            P("dom", None),
            P(),
            P(),
            P(),
            P(),
            P("dom", None),
            P("dom", None),
            P("dom"),
            P("dom"),
            P("dom"),
            P("dom", None),
        ),
        out_specs=(P("dom", None), P("dom", None), P(), P(), P(), P()),
        check_vma=False,
    )
```

```python
import functools

import jax
import jax.numpy as jnp
from jax import lax
from jax.experimental import pallas as pl
from jax.experimental.pallas import tpu as pltpu
from jax.sharding import PartitionSpec as P

BF = jnp.bfloat16
F32 = jnp.float32
MIB = 1 << 20
HALO_WIDTHS = (512, 512)
TILES = 2
ROWS = 256
LAST = ("q", "p")
ORDER = (
    "K", "O", "d0", "d1", "G", "d0", "d1", "H", "B", "d0", "d1", "t", "h", "d0", "d1", "b", "t",
    "h", "d0", "d1", "t", "h", "x0", "e", "t", "p0", "h", "x1", "p1", "t", "R", "t", "F", "P",
)

FREE = pl.CostEstimate(flops=0, bytes_accessed=0, transcendentals=0)
LARGE = pl.CostEstimate(flops=4_600_000_000, bytes_accessed=0, transcendentals=0)
HBM = pl.BlockSpec(memory_space=pltpu.HBM)
SMEM = pl.BlockSpec(memory_space=pltpu.SMEM)
VMEM = pl.BlockSpec(memory_space=pltpu.VMEM)
BY_ROWS = (((0,), (0,)), ((), ()))


def shape_of(shape, dtype):
    return jax.ShapeDtypeStruct(shape, dtype)


def far_shape(shape, dtype):
    return pltpu.HBM(shape, dtype)


def call(body, out_shape, name, vmem=24, cost=FREE, **rest):
    kernel = pl.pallas_call(
        body,
        out_shape=out_shape,
        compiler_params=pltpu.CompilerParams(vmem_limit_bytes=vmem * MIB),
        cost_estimate=cost,
        name=name,
        **rest,
    )
    specs = rest.get("in_specs")

    def run(*operands):
        if specs is None:
            return kernel(*operands)
        return kernel(
            *[
                pltpu.with_memory_space_constraint(x, pltpu.HBM) if spec is HBM else x
                for x, spec in zip(operands, specs)
            ]
        )

    return run


def scalars(*x):
    return jnp.stack([jnp.int32(v) for v in x])


def mxu(a, b):
    return jnp.dot(a, b, preferred_element_type=F32)


def by_rows(a, b):
    return lax.dot_general(a, b, BY_ROWS, preferred_element_type=F32)


def copy_all(copies):
    for c in copies:
        c.start()
    for c in copies:
        c.wait()


def tick_kernel(x, out):
    out[...] = x[...]


def tick_of(x):
    return call(tick_kernel, shape_of(x.shape, x.dtype), "tick", cost=LARGE)(x)


def outgoing_kernel(where, rows, features, away, *keep):
    nodes, width = features.shape
    half = width // 2
    hot = (rows[...] == lax.broadcasted_iota(jnp.int32, (rows.shape[0], nodes), 1)).astype(BF)
    there = features[:, pl.ds(pl.multiple_of((1 - where[0]) * half, half), half)]
    away[...] = mxu(hot, there).astype(BF)
    here = mxu(hot, features[:, pl.ds(pl.multiple_of(where[0] * half, half), half)]).astype(BF)
    at = 0
    for out in keep:
        out[...] = here[:, at : at + out.shape[1]]
        at += out.shape[1]


def outgoing_rows(core, rows, features, widths):
    sends, half = rows.shape[0], features.shape[1] // 2
    return call(
        outgoing_kernel,
        tuple(shape_of((sends, w), BF) for w in (half,) + widths),
        "outgoing",
        in_specs=[SMEM, VMEM, VMEM],
    )(scalars(core), rows, features)


def stack_kernel(n, received, *refs):
    own, outs = refs[:n], refs[n:]
    at = 0
    for x, out in zip(own, outs):
        rows, w = x.shape
        out[:rows, :] = x[...]
        out[rows:, :] = received[:, at : at + w]
        at += w


def stack(own, received):
    return call(
        functools.partial(stack_kernel, len(own)),
        tuple(shape_of((2 * x.shape[0], x.shape[1]), BF) for x in own),
        "stack",
    )(received, *own)


def stack_rows_kernel(own, received, out):
    rows = own.shape[0]
    out[:rows, :] = own[...]
    out[rows:, :] = received[...]


def stack_rows(own, received):
    rows, w = own.shape
    return call(stack_rows_kernel, shape_of((2 * rows, w), own.dtype), "stack_rows")(
        own, received
    )


def counts_kernel(packed, label, halo_count, own_count, factors):
    nodes, columns = packed.shape
    slots = columns - 1

    def count(labels):
        total = jnp.zeros((nodes, labels.shape[1]), F32)
        for e in range(slots):
            total = total + jnp.where(packed[:, e : e + 1] == labels, 1.0, 0.0)
        return total

    halo_count[...] = count(label[...]).astype(BF)
    local = lax.broadcasted_iota(jnp.int32, (nodes, nodes), 1)
    row = lax.broadcasted_iota(jnp.int32, (nodes, nodes), 0)
    own_count[...] = (count(local) + jnp.where(row == local, 2.0, 0.0)).astype(BF)
    degree = jnp.zeros((nodes, 1), F32)
    for e in range(slots):
        degree = degree + jnp.where(packed[:, e : e + 1] >= 0, 1.0, 0.0)
    lane = lax.broadcasted_iota(jnp.int32, factors.shape, 1)
    factors[...] = jnp.where(lane == 0, packed[:, slots:].astype(F32), 1.0 / (degree + 1.0))


def counts(packed, label):
    nodes = packed.shape[0]
    return call(
        counts_kernel,
        (
            shape_of((nodes, label.shape[1]), BF),
            shape_of((nodes, nodes), BF),
            shape_of((nodes, 128), F32),
        ),
        "counts",
    )(packed, label)


def aggregate_kernel(n, where, features, features_in, *refs):
    own, sibling, halos = refs[:3], refs[3:6], refs[6 : 6 + n]
    out, near, sem = refs[6 + n :]
    _, nodes, half = near.shape
    core = where[0]
    here = pl.ds(pl.multiple_of(core * half, half), half)
    copies = [
        pltpu.make_async_copy(x.at[:, here], near.at[k], sem.at[k])
        for k, x in enumerate((features, features_in))
    ]
    for c in copies:
        c.start()
    for k, (halo_count, own_count, factors) in enumerate((own, sibling)):
        rows = pl.ds(pl.multiple_of((core if k == 0 else 1 - core) * nodes, nodes), nodes)
        start = 0
        for i, halo in enumerate(halos):
            part = slice(start, start + halo.shape[1])
            total = mxu(halo_count[...], halo[...])
            if i == 0:
                copies[k].wait()
            total = total + mxu(own_count[...], near[k][:, part])
            out[rows, part] = (total * factors[:, 1:2]).astype(BF)
            start += halo.shape[1]


def aggregate(core, features, features_in, own, sibling, halos):
    rows, width = features.shape
    half = width // 2
    return call(
        functools.partial(aggregate_kernel, len(halos)),
        shape_of((2 * rows, half), BF),
        "aggregate",
        in_specs=[SMEM, HBM, HBM] + [VMEM] * (6 + len(halos)),
        scratch_shapes=[pltpu.VMEM((2, rows, half), BF), pltpu.SemaphoreType.DMA((2,))],
    )(scalars(core), features, features_in, *own, *sibling, *halos)


def grad_loads(core, cotangent, cotangent_in, near_g, column, sems):
    rows, width = cotangent.shape
    start, size = column
    whole = pl.ds(pl.multiple_of(core * (width // 2) + start, 256), size)
    own = pl.ds(pl.multiple_of(core * rows, rows), rows)
    far = pl.ds(pl.multiple_of((1 - core) * rows, rows), rows)
    return [
        pltpu.make_async_copy(cotangent.at[:, whole], near_g.at[own, :], sems.at[0]),
        pltpu.make_async_copy(cotangent_in.at[:, whole], near_g.at[far, :], sems.at[1]),
    ]


def factor(core, own, other, lane):
    return jnp.concatenate(
        [jnp.where(core == k, own[:, lane : lane + 1], other[:, lane : lane + 1]) for k in range(2)], 0
    )


def forward_kernel(
    where, mine, other, constants, own_factors, other_factors,
    weight, cotangent, cotangent_in,
    z_out, stats_ref, near_mine, near_other, near_g, z_ref, sem, out_sem,
):
    core = where[0]
    block = 256
    half = z_ref.shape[1]
    own = pl.ds(pl.multiple_of(core * half, half), half)
    far = pl.ds(pl.multiple_of((1 - core) * half, half), half)

    def loads(k, start, size):
        whole = pl.ds(pl.multiple_of(core * half + start, 256), size)
        part = slice(start, start + size)
        return [
            pltpu.make_async_copy(weight.at[own, whole], near_mine.at[:, part], sem.at[0, k]),
            pltpu.make_async_copy(weight.at[far, whole], near_other.at[:, part], sem.at[1, k]),
        ]

    ranges = ((0, block), (block, half - block))
    copies = [loads(k, *r) for k, r in enumerate(ranges)]
    grads = grad_loads(core, cotangent, cotangent_in, near_g, (0, half), sem.at[2])
    for c in copies[0] + grads + copies[1]:
        c.start()

    def store(j):
        part = slice(2 * j * block, 2 * (j + 1) * block)
        return pltpu.make_async_copy(z_ref.at[:, part], z_out.at[:, part], out_sem.at[j])

    valid = factor(core, own_factors, other_factors, 0)
    bias = constants[0:1, own]
    for j in range(half // block):
        at = slice(j * block, (j + 1) * block)
        if j < 2:
            for c in copies[j]:
                c.wait()
        for k in range(z_ref.shape[0] // ROWS):
            rows = slice(k * ROWS, (k + 1) * ROWS)
            z = mxu(mine[rows, :], near_mine[:, at]) + mxu(other[rows, :], near_other[:, at])
            z_ref[rows, at] = z + bias[:, at]
        if j == 0:
            for c in grads:
                c.wait()
        if j % 2 == 1:
            store(j // 2).start()
        z = z_ref[:, at]
        sigma = 1.0 / (1.0 + jnp.exp(-z))
        y = z * sigma
        slope = (sigma + y * (1.0 - sigma)) * valid
        g = near_g[:, at].astype(F32) * valid

        def column(x):
            return jnp.sum(x, axis=0, keepdims=True)

        count = jnp.broadcast_to(column(valid), (1, block))
        y_sum = column(y * valid)
        centred = (y - y_sum / jnp.maximum(count, 1.0)) * valid
        stats_ref[0:1, at] = count
        stats_ref[1:2, at] = y_sum
        stats_ref[2:3, at] = column(centred * centred)
        stats_ref[3:4, at] = column(g)
        stats_ref[4:5, at] = column(g * centred)
        stats_ref[5:6, at] = column(slope * g)
        stats_ref[6:7, at] = column(slope)
        stats_ref[7:8, at] = column(slope * centred)
    for j in range(half // block // 2):
        store(j).wait()


def forward(core, mine, other, weight, constants, cotangent, cotangent_in, own, sibling):
    rows, half = cotangent.shape[0], mine.shape[1]
    return call(
        forward_kernel,
        (far_shape((2 * rows, half), F32), shape_of((8, half), F32)),
        "forward",
        in_specs=[SMEM] + [VMEM] * 5 + [HBM] * 3,
        out_specs=(HBM, VMEM),
        scratch_shapes=[
            pltpu.VMEM((half, half), BF),
            pltpu.VMEM((half, half), BF),
            pltpu.VMEM((2 * rows, half), BF),
            pltpu.VMEM((2 * rows, half), F32),
            pltpu.SemaphoreType.DMA((3, 2)),
            pltpu.SemaphoreType.DMA((half // 512,)),
        ],
    )(
        scalars(core), mine, other, constants, own, sibling, weight, cotangent, cotangent_in
    )


def merge_kernel(where, own, received, out):
    upper = where[0] == 1
    a, b = own[...], received[...]
    a, b = jnp.where(upper, b, a), jnp.where(upper, a, b)

    def row(x, k):
        return x[k : k + 1, :]

    na, nb = row(a, 0), row(b, 0)
    n = na + nb
    mean = (row(a, 1) + row(b, 1)) / jnp.maximum(n, 1.0)
    da = row(a, 1) / jnp.maximum(na, 1.0) - mean
    db = row(b, 1) / jnp.maximum(nb, 1.0) - mean
    out[...] = a + b
    out[2:3, :] = (row(a, 2) + na * da * da) + (row(b, 2) + nb * db * db)
    out[4:5, :] = (row(a, 4) + da * row(a, 3)) + (row(b, 4) + db * row(b, 3))
    out[7:8, :] = (row(a, 7) + da * row(a, 6)) + (row(b, 7) + db * row(b, 6))


def merge(own, received, v):
    return call(
        merge_kernel, shape_of(own.shape, F32), "merge", in_specs=[SMEM, VMEM, VMEM]
    )(scalars(v), own, received)


def gradient(where, at, stats_ref, constants, z, g_in, valid):
    core, half, start = where
    size = z.shape[1]
    vector = pl.ds(pl.multiple_of(core * half + start, size), size)
    stats = stats_ref[:, at]
    gamma, beta = constants[1:2, vector], constants[2:3, vector]
    n = stats[0:1, :]
    mean = stats[1:2, :] / n
    deviation = lax.rsqrt(stats[2:3, :] / n + 1e-05)
    shift = stats[3:4, :]
    scale = deviation * stats[4:5, :]
    gain = gamma * deviation
    vectors = (
        gain * (stats[5:6, :] - shift / n * stats[6:7, :] - deviation * scale / n * stats[7:8, :]),
        scale,
        shift,
    )
    sigma = 1.0 / (1.0 + jnp.exp(-z))
    y = z * sigma
    slope = (sigma + y * (1.0 - sigma)) * valid
    g = g_in.astype(F32) * valid
    normalized = (y - mean) * deviation
    dz = gain * (g - shift / n - normalized * (scale / n)) * slope
    return dz, valid * (gamma * normalized + beta), vectors


def dz_kernel(
    where, stats_ref, constants, own_factors, other_factors, z_ref, cotangent, cotangent_in,
    out, near_z, near_g, sem,
):
    side, core = where[0], where[1]
    half, size = z_ref.shape[1], out.shape[1]
    block = 256
    blocks = size // block

    def loads(k):
        start = side * size + k * block
        part = pl.ds(pl.multiple_of(start, block), block)
        here = slice(k * block, (k + 1) * block)
        copy = pltpu.make_async_copy(z_ref.at[:, part], near_z.at[:, here], sem.at[k, 2])
        return [copy] + grad_loads(
            core, cotangent, cotangent_in, near_g.at[:, here], (start, block), sem.at[k]
        )

    copies = [loads(k) for k in range(blocks)]
    for c in copies[0] + copies[1]:
        c.start()
    valid = factor(core, own_factors, other_factors, 0)
    for k in range(blocks):
        for c in copies[k]:
            c.wait()
        here = slice(k * block, (k + 1) * block)
        start = side * size + k * block
        at = pl.ds(pl.multiple_of(start, block), block)
        dz, _, _ = gradient(
            (core, half, start), at, stats_ref, constants, near_z[:, here], near_g[:, here], valid
        )
        out[:, here] = dz.astype(BF)


def dz_of(core, side, z, stats, constants, cotangent, cotangent_in, own, sibling):
    rows, half = z.shape
    return call(
        dz_kernel,
        shape_of((rows, half // 2), BF),
        "dz",
        in_specs=[SMEM] + [VMEM] * 4 + [HBM] * 3,
        scratch_shapes=[
            pltpu.VMEM((rows, half // 2), F32),
            pltpu.VMEM((rows, half // 2), BF),
            pltpu.SemaphoreType.DMA((2, 3)),
        ],
    )(scalars(side, core), stats, constants, own, sibling, z, cotangent, cotangent_in)


def outputs_kernel(
    where, stats_ref, constants, own_factors, other_factors, z_ref, cotangent, cotangent_in,
    dz_scaled, act_keep, act_away, vectors, near_z, near_g, sem,
):
    core = where[0]
    rows, half = z_ref.shape
    nodes = rows // 2
    block = 256
    copies = [pltpu.make_async_copy(z_ref, near_z, sem.at[2])]
    copies += grad_loads(core, cotangent, cotangent_in, near_g, (0, half), sem)
    for c in copies:
        c.start()
    valid, inverse = (factor(core, own_factors, other_factors, lane) for lane in range(2))
    for c in copies:
        c.wait()
    vectors[3:8, :] = jnp.zeros((5, half), F32)
    for k in range(half // block):
        at = slice(k * block, (k + 1) * block)
        dz, act, sums = gradient(
            (core, half, k * block), at, stats_ref, constants, near_z[:, at], near_g[:, at], valid
        )
        dz_scaled[:, at] = (dz * inverse).astype(BF)
        act = act.astype(BF)
        act_keep[:, at] = jnp.where(core == 0, act[:nodes], act[nodes:])
        act_away[:, at] = jnp.where(core == 0, act[nodes:], act[:nodes])
        for i, x in enumerate(sums):
            vectors[i : i + 1, at] = x


def outputs(core, z, stats, constants, cotangent, cotangent_in, own, sibling):
    rows, half = z.shape
    act = shape_of((rows // 2, half), BF)
    return call(
        outputs_kernel,
        (shape_of((rows, half), BF), act, act, shape_of((8, half), F32)),
        "outputs",
        in_specs=[SMEM] + [VMEM] * 4 + [HBM] * 3,
        scratch_shapes=[
            pltpu.VMEM((rows, half), F32),
            pltpu.VMEM((rows, half), BF),
            pltpu.SemaphoreType.DMA((3,)),
        ],
    )(scalars(core), stats, constants, own, sibling, z, cotangent, cotangent_in)


def fetch_kernel(where, mine, other, mine_pair, other_pair, out, out_pair, sem):
    for flag, pair in ((1, (mine, mine_pair)), (0, (other, other_pair))):

        @pl.when(where[0] == flag)
        def _():
            copy_all(
                [
                    pltpu.make_async_copy(x, o, sem.at[i])
                    for i, (x, o) in enumerate(zip(pair, (out, out_pair)))
                ]
            )


def fetch(flag, mine, other, mine_pair, other_pair):
    out = shape_of(mine.shape, mine.dtype)
    return call(
        fetch_kernel,
        (out, out),
        "fetch",
        in_specs=[SMEM] + [HBM] * 4,
        out_specs=(VMEM, VMEM),
        scratch_shapes=[pltpu.SemaphoreType.DMA((2,))],
    )(scalars(flag), mine, other, mine_pair, other_pair)


def weight_part_kernel(columns, agg, agg_pair, dz, dz_pair, out):
    out[...] = (
        by_rows(agg[:, columns], dz[...]) + by_rows(agg_pair[:, columns], dz_pair[...])
    ).astype(BF)


def weight_part(agg, agg_pair, dz, dz_pair, t):
    tall = agg.shape[1] // TILES
    return call(
        functools.partial(weight_part_kernel, slice(t * tall, (t + 1) * tall)),
        shape_of((tall, dz.shape[1]), BF),
        "weight_part",
    )(agg, agg_pair, dz, dz_pair)


def fold_kernel(where, own, received, away, keep):
    rows = keep.shape[0]
    for side, out in ((1 - where[0], away), (where[0], keep)):
        part = pl.ds(pl.multiple_of(side * rows, rows), rows)
        out[...] = (own[part, :].astype(F32) + received[part, :].astype(F32)).astype(BF)


def fold(own, received, v):
    rows, w = own.shape
    out = shape_of((rows // 2, w), BF)
    return call(fold_kernel, (out, out), "fold", in_specs=[SMEM, VMEM, VMEM])(
        scalars(v), own, received
    )


def total_kernel(own, received, out):
    out[...] = (own[...].astype(F32) + received[...].astype(F32)).astype(BF)


def total_of(own, received):
    return call(total_kernel, shape_of(own.shape, BF), "total")(own, received)


def join_kernel(where, own, received, out):
    rows = own.shape[0]
    for side, x in ((where[0], own), (1 - where[0], received)):
        out[pl.ds(pl.multiple_of(side * rows, rows), rows), :] = x[...]


def join(own, received, v):
    rows, w = own.shape
    return call(
        join_kernel,
        shape_of((2 * rows, w), BF),
        "join",
        in_specs=[SMEM, VMEM, VMEM],
    )(scalars(v), own, received)


def place_kernel(n, where, *refs):
    pieces, (out, wide, put) = refs[:n], refs[-3:]

    def write(i, k):
        rows, w = pieces[i].shape
        row = pl.multiple_of(where[3 * i + k], 64)
        column = pl.multiple_of(where[3 * i + 2], 128)
        return pltpu.make_async_copy(
            wide.at[i, k * (rows // 2) : (k + 1) * (rows // 2), :],
            out.at[pl.ds(row, rows // 2), pl.ds(column, w)],
            put.at[i, k],
        )

    for i in range(n):
        step = 128
        half = pieces[i].shape[0] // 2
        for k in range(2):

            @pl.loop(0, half // step)
            def _(j):
                part = pl.ds(pl.multiple_of(k * half + j * step, step), step)
                wide[i, part, :] = pieces[i][part, :].astype(F32)

            write(i, k).start()
    for i in range(n):
        for k in range(2):
            write(i, k).wait()


def place(total, pieces, shape):
    n = len(pieces)
    rows, w = pieces[0][0].shape
    operands = [scalars(*[x for p in pieces for x in p[1:]])] + [p[0] for p in pieces]
    specs = [SMEM] + [VMEM] * n
    aliases = {}
    if total is not None:
        aliases = {len(operands): 0}
        operands.append(total)
        specs.append(HBM)
    return call(
        functools.partial(place_kernel, n),
        far_shape(shape, F32),
        "place",
        in_specs=specs,
        out_specs=HBM,
        scratch_shapes=[pltpu.VMEM((n, rows, w), F32), pltpu.SemaphoreType.DMA((n, 2))],
        input_output_aliases=aliases,
    )(*operands)


def back_part_kernel(columns, where, own, sibling, dz, out):
    nodes = own.shape[0]
    total = 0.0
    for side, count in ((where[0], own), (1 - where[0], sibling)):
        rows = pl.ds(pl.multiple_of(side * nodes, nodes), nodes)
        total = total + by_rows(count[:, columns], dz[rows, :])
    out[...] = total.astype(BF)


def back_part(core, own, sibling, dz, k, parts):
    rows = own.shape[1] // parts
    return call(
        functools.partial(back_part_kernel, slice(k * rows, (k + 1) * rows)),
        shape_of((rows, dz.shape[1]), BF),
        "back_part",
        in_specs=[SMEM] + [VMEM] * 3,
    )(scalars(core), own, sibling, dz)


def halve_kernel(own, received, away, keep):
    rows = keep.shape[0]
    keep[...] = (own[:rows].astype(F32) + received[:rows].astype(F32)).astype(BF)
    away[...] = (own[rows:].astype(F32) + received[rows:].astype(F32)).astype(BF)


def halve(own, received):
    rows, w = own.shape
    out = shape_of((rows // 2, w), BF)
    return call(halve_kernel, (out, out), "halve")(own, received)


def own_back_kernel(where, own, sibling, dz, keep, away):
    nodes = keep.shape[0]
    core = where[0]
    for side, count, out in ((core, own, keep), (1 - core, sibling, away)):
        part = pl.ds(pl.multiple_of(side * nodes, nodes), nodes)
        out[...] = by_rows(count[...], dz[part, :]).astype(BF)


def own_back(core, own, sibling, dz):
    rows, half = dz.shape
    out = shape_of((rows // 2, half), BF)
    return call(own_back_kernel, (out, out), "own_back", in_specs=[SMEM] + [VMEM] * 3)(
        scalars(core), own, sibling, dz
    )


def finish_kernel(
    where, rows, back, back_in, vec, vec_in, own, own_in, act, act_in, weight,
    grad, activations, vectors, near_weight, near_own, table, weight_sem, own_sem, act_sem,
):
    core = where[0]
    nodes, half = own.shape
    sends = rows.shape[0]
    block = 512
    blocks = weight.shape[0] // block

    def side_of(k):
        return pl.ds(pl.multiple_of((core if k == 0 else 1 - core) * half, half), half)

    owns = [
        pltpu.make_async_copy(x, near_own.at[k], own_sem.at[k]) for k, x in enumerate((own, own_in))
    ]
    acts = [
        pltpu.make_async_copy(x, activations.at[:, side_of(k)], act_sem.at[k])
        for k, x in enumerate((act, act_in))
    ]
    weights = [
        pltpu.make_async_copy(
            weight.at[k * block : (k + 1) * block, :],
            near_weight.at[k * block : (k + 1) * block, :],
            weight_sem.at[k],
        )
        for k in range(blocks)
    ]
    for c in owns + weights + acts:
        c.start()
    hot = (rows[...] == lax.broadcasted_iota(jnp.int32, (sends, nodes), 1)).astype(BF)
    for k, (back_part, vector) in enumerate(((back[:sends], vec), (back_in[...], vec_in))):
        vectors[:, side_of(k)] = vector[...]
        owns[k].wait()
        part = near_own[k].astype(F32) + by_rows(hot, back_part)
        table[:, side_of(k)] = part.astype(BF)
    for k in range(blocks):
        weights[k].wait()
        part = slice(k * block, (k + 1) * block)
        grad[:, part] = lax.dot_general(
            table[...], near_weight[part, :], (((1,), (1,)), ((), ())), preferred_element_type=F32
        ).astype(BF)
    for c in acts:
        c.wait()


def finish(core, rows, back, back_in, own, own_in, act, act_in, vec, vec_in, weight):
    nodes, half = own.shape
    width = 2 * half
    return call(
        finish_kernel,
        (
            shape_of((nodes, width), BF),
            shape_of((nodes, width), BF),
            shape_of((8, width), F32),
        ),
        "finish",
        in_specs=[SMEM] + [VMEM] * 5 + [HBM] * 5,
        out_specs=(VMEM, VMEM, VMEM),
        scratch_shapes=[
            pltpu.VMEM(weight.shape, BF),
            pltpu.VMEM((2, nodes, half), BF),
            pltpu.VMEM((nodes, width), BF),
            pltpu.SemaphoreType.DMA((width // 512,)),
            pltpu.SemaphoreType.DMA((2,)),
            pltpu.SemaphoreType.DMA((2,)),
        ],
    )(scalars(core), rows, back, back_in, vec, vec_in, own, own_in, act, act_in, weight)


def on_device(
    size,
    features,
    weight,
    bias,
    gamma,
    beta,
    neighbours,
    edge_mask,
    node_mask,
    send_rows,
    send_mask,
    cotangent,
):
    nodes, width = features.shape
    sends = send_rows.shape[0]
    half = width // 2
    quarter = width // 4
    levels = size.bit_length() - 5

    me = lax.axis_index("dom")
    core = me & 1
    is0 = core == 0
    bits = {"f": (1, 2), "p": (2, 3), "q": (3, 1), "s": (2, 1), "z": (3, 3)}
    others = list(range(4, levels + 4))
    for b in others:
        bits[b] = (b, b)
    axes = ["f", "p", "q"] + others

    def bit_of(b):
        return (me >> b) & 1

    def bit(b):
        return jnp.where(is0, bit_of(bits[b][0]), bit_of(bits[b][1]))

    def weight_of(b):
        return jnp.where(is0, 1 << bits[b][0], 1 << bits[b][1])

    def peer(i, b):
        return i ^ (1 << bits[b][i & 1])

    first, sibling_first = bit("f"), jnp.where(is0, bit_of(2), bit_of(1))
    high, sibling_high = bit("p"), jnp.where(is0, bit_of(3), bit_of(2))

    def along(x, b):
        return lax.ppermute(x, "dom", [(i, peer(i, b)) for i in range(size)])

    def swap(x):
        return lax.ppermute(x, "dom", [(i, i ^ 1) for i in range(size)])

    token = [jnp.zeros((8, 128), F32)]

    def arrive(*x):
        *x, token[0] = lax.optimization_barrier((*x, token[0]))
        return x[0] if len(x) == 1 else x

    def tick():
        token[0] = tick_of(token[0])

    def start(generators):
        running = dict(generators)
        for k in running:
            next(running[k])
        done = {}

        def advance(k):
            try:
                next(running[k])
            except StopIteration as stop:
                done[k] = stop.value

        return advance, done

    live_row = jnp.where(send_mask > 0, send_rows, -1)[:, None]
    out_away, *out_keep = outgoing_rows(
        core, live_row, features, HALO_WIDTHS
    )
    outgoing = stack(out_keep, arrive(swap(out_away)))
    halo_rows = sends * size
    chip_rows = 2 * sends

    def gather_halo(x):
        for b in reversed(axes):
            received = along(x, b)
            yield
            x = stack_rows(x, arrive(received))
        return x

    generators = {k: gather_halo(x) for k, x in enumerate(outgoing)}
    advance, halo = start(generators)

    def hop():
        for k in generators:
            advance(k)

    live_neighbour = jnp.where(edge_mask > 0, neighbours, -1)
    packed = jnp.concatenate([live_neighbour, node_mask[:, None]], 1)
    place_of = jnp.arange(halo_rows)
    chip, row = place_of // chip_rows, place_of % chip_rows
    relative = 0
    for k, b in enumerate(axes):
        relative = relative + ((chip >> (len(axes) - 1 - k)) & 1) * weight_of(b)
    owner = (me ^ relative) ^ (row // sends)
    label = (nodes + owner * sends + row % sends)[None, :]
    packed, label = arrive(packed, label)
    sibling_packed = arrive(swap(packed))
    hop()
    features_in, cotangent_in = swap(features), swap(cotangent)
    constants = jnp.stack([bias, gamma, beta])
    packed = arrive(packed)
    own = arrive(*counts(packed, label))
    constants = arrive(constants)
    hop()
    features_in, cotangent_in, sibling_packed = arrive(features_in, cotangent_in, sibling_packed)
    sibling = arrive(*counts(sibling_packed, label))
    hop()
    for _ in range(levels):
        hop()

    agg_mine = aggregate(
        core, features, features_in, own, sibling, [halo[k] for k in generators]
    )
    agg_other = swap(agg_mine)
    mine_pair = along(agg_mine, "f")
    agg_other = arrive(agg_other)
    other_pair = along(agg_other, "f")
    z, stats = forward(
        core, agg_mine, agg_other, weight, constants, cotangent, cotangent_in, own[2], sibling[2]
    )

    same = (high == core).astype(jnp.int32)
    for k, b in enumerate(others + ["q", "p", "f"]):
        received = along(stats, b)
        if k == 0:
            mine_pair = arrive(mine_pair)
        if b == "f":
            other_pair = arrive(other_pair)
        stats = merge(stats, arrive(received), bit(b))
    nodes_args = (z, stats, constants, cotangent, cotangent_in, own[2], sibling[2])
    dz_send = dz_of(core, 1 - first, *nodes_args)

    dz_pair = along(dz_send, "f")
    aggs = (agg_mine, agg_other, mine_pair, other_pair)
    dz_send = arrive(dz_send)
    dz_keep = dz_of(core, first, *nodes_args)
    away = fetch(1 - same, *aggs)
    dz_keep, *away = arrive(dz_keep, *away)
    dz_pair = arrive(dz_pair)

    def weight_gradient(t):
        received = along(weight_part(*away, dz_keep, dz_pair, t), "p")
        yield
        part = weight_part(*keep, dz_keep, dz_pair, t)
        part = arrive(part)
        yield
        received = arrive(received)
        for b in axes[2:]:
            out, part = fold(part, received, bit(b))
            received = along(out, b)
            yield
            received = arrive(received)
        part = total_of(part, received)
        for b in others[::-1] + [LAST[0]]:
            received = along(part, b)
            yield
            part = join(part, arrive(received), bit(b))
        return part

    def reduce_halo():
        received, part = along(back_send, axes[0]), back_keep
        for b in axes[1:]:
            yield
            out, part = halve(part, arrive(received))
            received = along(out, b)
        yield
        return total_of(part, arrive(received))

    generators = {"d%d" % t: weight_gradient(t) for t in range(TILES)}
    advance, found = start(generators)
    groups = {k: [1, 1, len(others), len(others), 1] for k in generators}
    groups["h"] = [1, 1, 1, len(others)]
    tall = half // TILES
    tiles = range(TILES)
    shape = (width, width)
    if LAST[1] == "z":
        layers = bit_of(3), bit_of(3)
        steps = jnp.where(is0, half, tall // 2), jnp.where(is0, tall // 2, half)
        steps = steps, steps[::-1]
    else:
        layers = high, sibling_high
        steps = ((tall // 2, half),) * 2

    def pieces(own, sibling, away, other):
        placed = []
        for side, arrays in enumerate((own, sibling)):
            begin = core if side == 0 else 1 - core
            f = first if side == 0 else sibling_first
            inner, outer = steps[side]
            z = 1 - layers[side] if away else layers[side]
            for t, x in enumerate(arrays):
                row = t * tall + z * outer
                column = begin * half + (1 - f if other else f) * quarter
                placed.append((x, row, row + inner, column))
        return placed

    across, pair, here = [None] * TILES, [None] * TILES, [None] * TILES
    here_across, here_pair, pair_across = [None] * TILES, [None] * TILES, [None] * TILES
    for action in ORDER:
        if action == "K":
            keep = arrive(*fetch(same, *aggs))
            for k in generators:
                advance(k)
        elif action == "O":
            dz_scaled, act, act_away, vectors = arrive(*outputs(core, *nodes_args))
        elif action == "G":
            dz_scaled = arrive(dz_scaled)
            back_send, back_keep = arrive(
                *(back_part(core, own[0], sibling[0], dz_scaled, k, 2) for k in (1, 0))
            )
        elif action == "H":
            back_send = arrive(back_send)
            advance_halo, halo_part = start({"h": reduce_halo()})
        elif action == "B":
            dz_scaled = arrive(dz_scaled)
            kept_back, away_back = arrive(*own_back(core, own[1], sibling[1], dz_scaled))
            own_in, act_in, vectors_in = swap(away_back), swap(act_away), swap(vectors)
        elif action == "b":
            own_in, act_in, vectors_in = arrive(own_in, act_in, vectors_in)
        elif action == "t":
            tick()
        elif action in groups:
            step = advance_halo if action == "h" else advance
            for _ in range(groups[action].pop(0)):
                step(action)
            if action in found:
                t = list(generators).index(action)
                across[t], pair[t] = along(found[action], LAST[1]), along(found[action], "f")
                here[t] = swap(found[action])
        elif action == "e":
            here = [arrive(x) for x in here]
            part = [found[k] for k in generators]
            total = arrive(place(None, pieces(part, here, False, False), shape))
        elif action[0] == "x":
            t = int(action[1])
            across[t] = arrive(across[t])
            here_across[t], pair_across[t] = swap(across[t]), along(across[t], "f")
        elif action[0] == "p":
            t = int(action[1])
            pair[t] = arrive(pair[t])
            here_pair[t] = swap(pair[t])
        elif action == "R":
            back = halo_part["h"]
            back_in = arrive(swap(back[sends:]))
        elif action == "F":
            grad_features, activations, vectors = arrive(
                *finish(
                    core, live_row, back, back_in, kept_back, own_in, act, act_in, vectors, vectors_in, weight
                )
            )
        elif action == "P":
            here_across = [arrive(x) for x in here_across]
            here_pair = [arrive(x) for x in here_pair]
            total = place(
                total,
                pieces(across, here_across, True, False) + pieces(pair, here_pair, False, True),
                shape,
            )
            total = arrive(total)
    pair_across = [arrive(x) for x in pair_across]
    vectors = vectors + token[0][0, 0]
    here_pair_across = [swap(x) for x in pair_across]
    total = place(total, pieces(pair_across, here_pair_across, True, True), shape)
    return activations, grad_features, total, vectors[0], vectors[1], vectors[2]


def solution(mesh):
    size = mesh.shape["dom"]
    return jax.shard_map(
        functools.partial(on_device, size),
        mesh=mesh,
        in_specs=(
            P("dom", None),
            P(),
            P(),
            P(),
            P(),
            P("dom", None),
            P("dom", None),
            P("dom"),
            P("dom"),
            P("dom"),
            P("dom", None),
        ),
        out_specs=(P("dom", None), P("dom", None), P(), P(), P(), P()),
        check_vma=False,
    )
```

```python
import functools

import jax
import jax.numpy as jnp
from jax import lax
from jax.experimental import pallas as pl
from jax.experimental.pallas import tpu as pltpu
from jax.sharding import PartitionSpec as P

BF = jnp.bfloat16
F32 = jnp.float32
MIB = 1 << 20
HALO_WIDTHS = (512, 512)
TILES = 2
ROWS = 256
LAST = ("q", "p")
ORDER = (
    "K", "O", "d0", "d1", "G", "d0", "d1", "H", "B", "d0", "d1", "t", "h", "d0", "d1", "b", "t",
    "h", "d0", "d1", "t", "h", "x0", "e", "t", "p0", "h", "x1", "p1", "t", "R", "t", "F", "P",
)

FREE = pl.CostEstimate(flops=0, bytes_accessed=0, transcendentals=0)
LARGE = pl.CostEstimate(flops=4_600_000_000, bytes_accessed=0, transcendentals=0)
HBM = pl.BlockSpec(memory_space=pltpu.HBM)
SMEM = pl.BlockSpec(memory_space=pltpu.SMEM)
VMEM = pl.BlockSpec(memory_space=pltpu.VMEM)
BY_ROWS = (((0,), (0,)), ((), ()))


def shape_of(shape, dtype):
    return jax.ShapeDtypeStruct(shape, dtype)


def far_shape(shape, dtype):
    return pltpu.HBM(shape, dtype)


def call(body, out_shape, name, vmem=24, cost=FREE, **rest):
    kernel = pl.pallas_call(
        body,
        out_shape=out_shape,
        compiler_params=pltpu.CompilerParams(vmem_limit_bytes=vmem * MIB),
        cost_estimate=cost,
        name=name,
        **rest,
    )
    specs = rest.get("in_specs")

    def run(*operands):
        if specs is None:
            return kernel(*operands)
        return kernel(
            *[
                pltpu.with_memory_space_constraint(x, pltpu.HBM) if spec is HBM else x
                for x, spec in zip(operands, specs)
            ]
        )

    return run


def scalars(*x):
    return jnp.stack([jnp.int32(v) for v in x])


def mxu(a, b):
    return jnp.dot(a, b, preferred_element_type=F32)


def by_rows(a, b):
    return lax.dot_general(a, b, BY_ROWS, preferred_element_type=F32)


def copy_all(copies):
    for c in copies:
        c.start()
    for c in copies:
        c.wait()


def tick_kernel(x, out):
    out[...] = x[...]


def tick_of(x):
    return call(tick_kernel, shape_of(x.shape, x.dtype), "tick", cost=LARGE)(x)


def outgoing_kernel(where, rows, features, away, *keep):
    nodes, width = features.shape
    half = width // 2
    hot = (rows[...] == lax.broadcasted_iota(jnp.int32, (rows.shape[0], nodes), 1)).astype(BF)
    there = features[:, pl.ds(pl.multiple_of((1 - where[0]) * half, half), half)]
    away[...] = mxu(hot, there).astype(BF)
    here = mxu(hot, features[:, pl.ds(pl.multiple_of(where[0] * half, half), half)]).astype(BF)
    at = 0
    for out in keep:
        out[...] = here[:, at : at + out.shape[1]]
        at += out.shape[1]


def outgoing_rows(core, rows, features, widths):
    sends, half = rows.shape[0], features.shape[1] // 2
    return call(
        outgoing_kernel,
        tuple(shape_of((sends, w), BF) for w in (half,) + widths),
        "outgoing",
        in_specs=[SMEM, VMEM, VMEM],
    )(scalars(core), rows, features)


def stack_kernel(n, received, *refs):
    own, outs = refs[:n], refs[n:]
    at = 0
    for x, out in zip(own, outs):
        rows, w = x.shape
        out[:rows, :] = x[...]
        out[rows:, :] = received[:, at : at + w]
        at += w


def stack(own, received):
    return call(
        functools.partial(stack_kernel, len(own)),
        tuple(shape_of((2 * x.shape[0], x.shape[1]), BF) for x in own),
        "stack",
    )(received, *own)


def stack_rows_kernel(own, received, out):
    rows = own.shape[0]
    out[:rows, :] = own[...]
    out[rows:, :] = received[...]


def stack_rows(own, received):
    rows, w = own.shape
    return call(stack_rows_kernel, shape_of((2 * rows, w), own.dtype), "stack_rows")(
        own, received
    )


def counts_kernel(packed, label, halo_count, own_count, factors):
    nodes, columns = packed.shape
    slots = columns - 1

    def count(labels):
        total = jnp.zeros((nodes, labels.shape[1]), F32)
        for e in range(slots):
            total = total + jnp.where(packed[:, e : e + 1] == labels, 1.0, 0.0)
        return total

    halo_count[...] = count(label[...]).astype(BF)
    local = lax.broadcasted_iota(jnp.int32, (nodes, nodes), 1)
    row = lax.broadcasted_iota(jnp.int32, (nodes, nodes), 0)
    own_count[...] = (count(local) + jnp.where(row == local, 2.0, 0.0)).astype(BF)
    degree = jnp.zeros((nodes, 1), F32)
    for e in range(slots):
        degree = degree + jnp.where(packed[:, e : e + 1] >= 0, 1.0, 0.0)
    lane = lax.broadcasted_iota(jnp.int32, factors.shape, 1)
    factors[...] = jnp.where(lane == 0, packed[:, slots:].astype(F32), 1.0 / (degree + 1.0))


def counts(packed, label):
    nodes = packed.shape[0]
    return call(
        counts_kernel,
        (
            shape_of((nodes, label.shape[1]), BF),
            shape_of((nodes, nodes), BF),
            shape_of((nodes, 128), F32),
        ),
        "counts",
    )(packed, label)


def aggregate_kernel(n, where, features, features_in, *refs):
    own, sibling, halos = refs[:3], refs[3:6], refs[6 : 6 + n]
    out, near, sums, sem = refs[6 + n :]
    _, nodes, half = near.shape
    core = where[0]
    here = pl.ds(pl.multiple_of(core * half, half), half)
    copies = [
        pltpu.make_async_copy(x.at[:, here], near.at[k], sem.at[k])
        for k, x in enumerate((features, features_in))
    ]
    for c in copies:
        c.start()
    for k, (halo_count, _, _) in enumerate((own, sibling)):
        start = 0
        for halo in halos:
            sums[k, :, start : start + halo.shape[1]] = mxu(halo_count[...], halo[...])
            start += halo.shape[1]
    for k, (_, own_count, factors) in enumerate((own, sibling)):
        rows = pl.ds(pl.multiple_of((core if k == 0 else 1 - core) * nodes, nodes), nodes)
        copies[k].wait()
        total = sums[k] + mxu(own_count[...], near[k])
        out[rows, :] = (total * factors[:, 1:2]).astype(BF)


def aggregate(core, features, features_in, own, sibling, halos):
    rows, width = features.shape
    half = width // 2
    return call(
        functools.partial(aggregate_kernel, len(halos)),
        shape_of((2 * rows, half), BF),
        "aggregate",
        in_specs=[SMEM, HBM, HBM] + [VMEM] * (6 + len(halos)),
        scratch_shapes=[
            pltpu.VMEM((2, rows, half), BF),
            pltpu.VMEM((2, rows, half), F32),
            pltpu.SemaphoreType.DMA((2,)),
        ],
    )(scalars(core), features, features_in, *own, *sibling, *halos)


def grad_loads(core, cotangent, cotangent_in, near_g, column, sems):
    rows, width = cotangent.shape
    start, size = column
    whole = pl.ds(pl.multiple_of(core * (width // 2) + start, 256), size)
    own = pl.ds(pl.multiple_of(core * rows, rows), rows)
    far = pl.ds(pl.multiple_of((1 - core) * rows, rows), rows)
    return [
        pltpu.make_async_copy(cotangent.at[:, whole], near_g.at[own, :], sems.at[0]),
        pltpu.make_async_copy(cotangent_in.at[:, whole], near_g.at[far, :], sems.at[1]),
    ]


def factor(core, own, other, lane):
    return jnp.concatenate(
        [jnp.where(core == k, own[:, lane : lane + 1], other[:, lane : lane + 1]) for k in range(2)], 0
    )


def forward_kernel(
    where, mine, other, constants, own_factors, other_factors,
    weight, cotangent, cotangent_in,
    z_out, stats_ref, near_mine, near_other, near_g, z_ref, sem, out_sem,
):
    core = where[0]
    block = 256
    half = z_ref.shape[1]
    own = pl.ds(pl.multiple_of(core * half, half), half)
    far = pl.ds(pl.multiple_of((1 - core) * half, half), half)

    def loads(k, start, size):
        whole = pl.ds(pl.multiple_of(core * half + start, 256), size)
        part = slice(start, start + size)
        return [
            pltpu.make_async_copy(weight.at[own, whole], near_mine.at[:, part], sem.at[0, k]),
            pltpu.make_async_copy(weight.at[far, whole], near_other.at[:, part], sem.at[1, k]),
        ]

    ranges = ((0, block), (block, half - block))
    copies = [loads(k, *r) for k, r in enumerate(ranges)]
    grads = grad_loads(core, cotangent, cotangent_in, near_g, (0, half), sem.at[2])
    for c in copies[0] + grads + copies[1]:
        c.start()

    def store(j):
        part = slice(2 * j * block, 2 * (j + 1) * block)
        return pltpu.make_async_copy(z_ref.at[:, part], z_out.at[:, part], out_sem.at[j])

    valid = factor(core, own_factors, other_factors, 0)
    bias = constants[0:1, own]
    for j in range(half // block):
        at = slice(j * block, (j + 1) * block)
        if j < 2:
            for c in copies[j]:
                c.wait()
        for k in range(z_ref.shape[0] // ROWS):
            rows = slice(k * ROWS, (k + 1) * ROWS)
            z = mxu(mine[rows, :], near_mine[:, at]) + mxu(other[rows, :], near_other[:, at])
            z_ref[rows, at] = z + bias[:, at]
        if j == 0:
            for c in grads:
                c.wait()
        if j % 2 == 1:
            store(j // 2).start()
        z = z_ref[:, at]
        sigma = 1.0 / (1.0 + jnp.exp(-z))
        y = z * sigma
        slope = (sigma + y * (1.0 - sigma)) * valid
        g = near_g[:, at].astype(F32) * valid

        def column(x):
            return jnp.sum(x, axis=0, keepdims=True)

        count = jnp.broadcast_to(column(valid), (1, block))
        y_sum = column(y * valid)
        centred = (y - y_sum / jnp.maximum(count, 1.0)) * valid
        stats_ref[0:1, at] = count
        stats_ref[1:2, at] = y_sum
        stats_ref[2:3, at] = column(centred * centred)
        stats_ref[3:4, at] = column(g)
        stats_ref[4:5, at] = column(g * centred)
        stats_ref[5:6, at] = column(slope * g)
        stats_ref[6:7, at] = column(slope)
        stats_ref[7:8, at] = column(slope * centred)
    for j in range(half // block // 2):
        store(j).wait()


def forward(core, mine, other, weight, constants, cotangent, cotangent_in, own, sibling):
    rows, half = cotangent.shape[0], mine.shape[1]
    return call(
        forward_kernel,
        (far_shape((2 * rows, half), F32), shape_of((8, half), F32)),
        "forward",
        in_specs=[SMEM] + [VMEM] * 5 + [HBM] * 3,
        out_specs=(HBM, VMEM),
        scratch_shapes=[
            pltpu.VMEM((half, half), BF),
            pltpu.VMEM((half, half), BF),
            pltpu.VMEM((2 * rows, half), BF),
            pltpu.VMEM((2 * rows, half), F32),
            pltpu.SemaphoreType.DMA((3, 2)),
            pltpu.SemaphoreType.DMA((half // 512,)),
        ],
    )(
        scalars(core), mine, other, constants, own, sibling, weight, cotangent, cotangent_in
    )


def merge_kernel(where, own, received, out):
    upper = where[0] == 1
    a, b = own[...], received[...]
    a, b = jnp.where(upper, b, a), jnp.where(upper, a, b)

    def row(x, k):
        return x[k : k + 1, :]

    na, nb = row(a, 0), row(b, 0)
    n = na + nb
    mean = (row(a, 1) + row(b, 1)) / jnp.maximum(n, 1.0)
    da = row(a, 1) / jnp.maximum(na, 1.0) - mean
    db = row(b, 1) / jnp.maximum(nb, 1.0) - mean
    out[...] = a + b
    out[2:3, :] = (row(a, 2) + na * da * da) + (row(b, 2) + nb * db * db)
    out[4:5, :] = (row(a, 4) + da * row(a, 3)) + (row(b, 4) + db * row(b, 3))
    out[7:8, :] = (row(a, 7) + da * row(a, 6)) + (row(b, 7) + db * row(b, 6))


def merge(own, received, v):
    return call(
        merge_kernel, shape_of(own.shape, F32), "merge", in_specs=[SMEM, VMEM, VMEM]
    )(scalars(v), own, received)


def gradient(where, at, stats_ref, constants, z, g_in, valid):
    core, half, start = where
    size = z.shape[1]
    vector = pl.ds(pl.multiple_of(core * half + start, size), size)
    stats = stats_ref[:, at]
    gamma, beta = constants[1:2, vector], constants[2:3, vector]
    n = stats[0:1, :]
    mean = stats[1:2, :] / n
    deviation = lax.rsqrt(stats[2:3, :] / n + 1e-05)
    shift = stats[3:4, :]
    scale = deviation * stats[4:5, :]
    gain = gamma * deviation
    vectors = (
        gain * (stats[5:6, :] - shift / n * stats[6:7, :] - deviation * scale / n * stats[7:8, :]),
        scale,
        shift,
    )
    sigma = 1.0 / (1.0 + jnp.exp(-z))
    y = z * sigma
    slope = (sigma + y * (1.0 - sigma)) * valid
    g = g_in.astype(F32) * valid
    normalized = (y - mean) * deviation
    dz = gain * (g - shift / n - normalized * (scale / n)) * slope
    return dz, valid * (gamma * normalized + beta), vectors


def dz_kernel(
    where, stats_ref, constants, own_factors, other_factors, z_ref, cotangent, cotangent_in,
    out, near_z, near_g, sem,
):
    side, core = where[0], where[1]
    half, size = z_ref.shape[1], out.shape[1]
    block = 256
    blocks = size // block

    def loads(k):
        start = side * size + k * block
        part = pl.ds(pl.multiple_of(start, block), block)
        here = slice(k * block, (k + 1) * block)
        copy = pltpu.make_async_copy(z_ref.at[:, part], near_z.at[:, here], sem.at[k, 2])
        return [copy] + grad_loads(
            core, cotangent, cotangent_in, near_g.at[:, here], (start, block), sem.at[k]
        )

    copies = [loads(k) for k in range(blocks)]
    for c in copies[0] + copies[1]:
        c.start()
    valid = factor(core, own_factors, other_factors, 0)
    for k in range(blocks):
        for c in copies[k]:
            c.wait()
        here = slice(k * block, (k + 1) * block)
        start = side * size + k * block
        at = pl.ds(pl.multiple_of(start, block), block)
        dz, _, _ = gradient(
            (core, half, start), at, stats_ref, constants, near_z[:, here], near_g[:, here], valid
        )
        out[:, here] = dz.astype(BF)


def dz_of(core, side, z, stats, constants, cotangent, cotangent_in, own, sibling):
    rows, half = z.shape
    return call(
        dz_kernel,
        shape_of((rows, half // 2), BF),
        "dz",
        in_specs=[SMEM] + [VMEM] * 4 + [HBM] * 3,
        scratch_shapes=[
            pltpu.VMEM((rows, half // 2), F32),
            pltpu.VMEM((rows, half // 2), BF),
            pltpu.SemaphoreType.DMA((2, 3)),
        ],
    )(scalars(side, core), stats, constants, own, sibling, z, cotangent, cotangent_in)


def outputs_kernel(
    where, stats_ref, constants, own_factors, other_factors, z_ref, cotangent, cotangent_in,
    dz_scaled, act_keep, act_away, vectors, near_z, near_g, sem,
):
    core = where[0]
    rows, half = z_ref.shape
    nodes = rows // 2
    block = 256
    copies = [pltpu.make_async_copy(z_ref, near_z, sem.at[2])]
    copies += grad_loads(core, cotangent, cotangent_in, near_g, (0, half), sem)
    for c in copies:
        c.start()
    valid, inverse = (factor(core, own_factors, other_factors, lane) for lane in range(2))
    for c in copies:
        c.wait()
    vectors[3:8, :] = jnp.zeros((5, half), F32)
    for k in range(half // block):
        at = slice(k * block, (k + 1) * block)
        dz, act, sums = gradient(
            (core, half, k * block), at, stats_ref, constants, near_z[:, at], near_g[:, at], valid
        )
        dz_scaled[:, at] = (dz * inverse).astype(BF)
        act = act.astype(BF)
        act_keep[:, at] = jnp.where(core == 0, act[:nodes], act[nodes:])
        act_away[:, at] = jnp.where(core == 0, act[nodes:], act[:nodes])
        for i, x in enumerate(sums):
            vectors[i : i + 1, at] = x


def outputs(core, z, stats, constants, cotangent, cotangent_in, own, sibling):
    rows, half = z.shape
    act = shape_of((rows // 2, half), BF)
    return call(
        outputs_kernel,
        (shape_of((rows, half), BF), act, act, shape_of((8, half), F32)),
        "outputs",
        in_specs=[SMEM] + [VMEM] * 4 + [HBM] * 3,
        scratch_shapes=[
            pltpu.VMEM((rows, half), F32),
            pltpu.VMEM((rows, half), BF),
            pltpu.SemaphoreType.DMA((3,)),
        ],
    )(scalars(core), stats, constants, own, sibling, z, cotangent, cotangent_in)


def fetch_kernel(where, mine, other, mine_pair, other_pair, out, out_pair, sem):
    for flag, pair in ((1, (mine, mine_pair)), (0, (other, other_pair))):

        @pl.when(where[0] == flag)
        def _():
            copy_all(
                [
                    pltpu.make_async_copy(x, o, sem.at[i])
                    for i, (x, o) in enumerate(zip(pair, (out, out_pair)))
                ]
            )


def fetch(flag, mine, other, mine_pair, other_pair):
    out = shape_of(mine.shape, mine.dtype)
    return call(
        fetch_kernel,
        (out, out),
        "fetch",
        in_specs=[SMEM] + [HBM] * 4,
        out_specs=(VMEM, VMEM),
        scratch_shapes=[pltpu.SemaphoreType.DMA((2,))],
    )(scalars(flag), mine, other, mine_pair, other_pair)


def weight_part_kernel(columns, agg, agg_pair, dz, dz_pair, out):
    out[...] = (
        by_rows(agg[:, columns], dz[...]) + by_rows(agg_pair[:, columns], dz_pair[...])
    ).astype(BF)


def weight_part(agg, agg_pair, dz, dz_pair, t):
    tall = agg.shape[1] // TILES
    return call(
        functools.partial(weight_part_kernel, slice(t * tall, (t + 1) * tall)),
        shape_of((tall, dz.shape[1]), BF),
        "weight_part",
    )(agg, agg_pair, dz, dz_pair)


def fold_kernel(where, own, received, away, keep):
    rows = keep.shape[0]
    for side, out in ((1 - where[0], away), (where[0], keep)):
        part = pl.ds(pl.multiple_of(side * rows, rows), rows)
        out[...] = (own[part, :].astype(F32) + received[part, :].astype(F32)).astype(BF)


def fold(own, received, v):
    rows, w = own.shape
    out = shape_of((rows // 2, w), BF)
    return call(fold_kernel, (out, out), "fold", in_specs=[SMEM, VMEM, VMEM])(
        scalars(v), own, received
    )


def total_kernel(own, received, out):
    out[...] = (own[...].astype(F32) + received[...].astype(F32)).astype(BF)


def total_of(own, received):
    return call(total_kernel, shape_of(own.shape, BF), "total")(own, received)


def join_kernel(where, own, received, out):
    rows = own.shape[0]
    for side, x in ((where[0], own), (1 - where[0], received)):
        out[pl.ds(pl.multiple_of(side * rows, rows), rows), :] = x[...]


def join(own, received, v):
    rows, w = own.shape
    return call(
        join_kernel,
        shape_of((2 * rows, w), BF),
        "join",
        in_specs=[SMEM, VMEM, VMEM],
    )(scalars(v), own, received)


def place_kernel(n, where, *refs):
    pieces, (out, wide, put) = refs[:n], refs[-3:]

    def write(i, k):
        rows, w = pieces[i].shape
        row = pl.multiple_of(where[3 * i + k], 64)
        column = pl.multiple_of(where[3 * i + 2], 128)
        return pltpu.make_async_copy(
            wide.at[i, k * (rows // 2) : (k + 1) * (rows // 2), :],
            out.at[pl.ds(row, rows // 2), pl.ds(column, w)],
            put.at[i, k],
        )

    for i in range(n):
        step = 128
        half = pieces[i].shape[0] // 2
        for k in range(2):

            @pl.loop(0, half // step)
            def _(j):
                part = pl.ds(pl.multiple_of(k * half + j * step, step), step)
                wide[i, part, :] = pieces[i][part, :].astype(F32)

            write(i, k).start()
    for i in range(n):
        for k in range(2):
            write(i, k).wait()


def place(total, pieces, shape):
    n = len(pieces)
    rows, w = pieces[0][0].shape
    operands = [scalars(*[x for p in pieces for x in p[1:]])] + [p[0] for p in pieces]
    specs = [SMEM] + [VMEM] * n
    aliases = {}
    if total is not None:
        aliases = {len(operands): 0}
        operands.append(total)
        specs.append(HBM)
    return call(
        functools.partial(place_kernel, n),
        far_shape(shape, F32),
        "place",
        in_specs=specs,
        out_specs=HBM,
        scratch_shapes=[pltpu.VMEM((n, rows, w), F32), pltpu.SemaphoreType.DMA((n, 2))],
        input_output_aliases=aliases,
    )(*operands)


def back_part_kernel(columns, where, own, sibling, dz, out):
    nodes = own.shape[0]
    total = 0.0
    for side, count in ((where[0], own), (1 - where[0], sibling)):
        rows = pl.ds(pl.multiple_of(side * nodes, nodes), nodes)
        total = total + by_rows(count[:, columns], dz[rows, :])
    out[...] = total.astype(BF)


def back_part(core, own, sibling, dz, k, parts):
    rows = own.shape[1] // parts
    return call(
        functools.partial(back_part_kernel, slice(k * rows, (k + 1) * rows)),
        shape_of((rows, dz.shape[1]), BF),
        "back_part",
        in_specs=[SMEM] + [VMEM] * 3,
    )(scalars(core), own, sibling, dz)


def halve_kernel(own, received, away, keep):
    rows = keep.shape[0]
    keep[...] = (own[:rows].astype(F32) + received[:rows].astype(F32)).astype(BF)
    away[...] = (own[rows:].astype(F32) + received[rows:].astype(F32)).astype(BF)


def halve(own, received):
    rows, w = own.shape
    out = shape_of((rows // 2, w), BF)
    return call(halve_kernel, (out, out), "halve")(own, received)


def own_back_kernel(where, own, sibling, dz, keep, away):
    nodes = keep.shape[0]
    core = where[0]
    for side, count, out in ((core, own, keep), (1 - core, sibling, away)):
        part = pl.ds(pl.multiple_of(side * nodes, nodes), nodes)
        out[...] = by_rows(count[...], dz[part, :]).astype(BF)


def own_back(core, own, sibling, dz):
    rows, half = dz.shape
    out = shape_of((rows // 2, half), BF)
    return call(own_back_kernel, (out, out), "own_back", in_specs=[SMEM] + [VMEM] * 3)(
        scalars(core), own, sibling, dz
    )


def finish_kernel(
    where, rows, back, back_in, vec, vec_in, own, own_in, act, act_in, weight,
    grad, activations, vectors, near_weight, near_own, table, weight_sem, own_sem, act_sem,
):
    core = where[0]
    nodes, half = own.shape
    sends = rows.shape[0]
    block = 512
    blocks = weight.shape[0] // block

    def side_of(k):
        return pl.ds(pl.multiple_of((core if k == 0 else 1 - core) * half, half), half)

    owns = [
        pltpu.make_async_copy(x, near_own.at[k], own_sem.at[k]) for k, x in enumerate((own, own_in))
    ]
    acts = [
        pltpu.make_async_copy(x, activations.at[:, side_of(k)], act_sem.at[k])
        for k, x in enumerate((act, act_in))
    ]
    weights = [
        pltpu.make_async_copy(
            weight.at[k * block : (k + 1) * block, :],
            near_weight.at[k * block : (k + 1) * block, :],
            weight_sem.at[k],
        )
        for k in range(blocks)
    ]
    for c in owns + weights + acts:
        c.start()
    hot = (rows[...] == lax.broadcasted_iota(jnp.int32, (sends, nodes), 1)).astype(BF)
    for k, (back_part, vector) in enumerate(((back[:sends], vec), (back_in[...], vec_in))):
        vectors[:, side_of(k)] = vector[...]
        owns[k].wait()
        part = near_own[k].astype(F32) + by_rows(hot, back_part)
        table[:, side_of(k)] = part.astype(BF)
    for k in range(blocks):
        weights[k].wait()
        part = slice(k * block, (k + 1) * block)
        grad[:, part] = lax.dot_general(
            table[...], near_weight[part, :], (((1,), (1,)), ((), ())), preferred_element_type=F32
        ).astype(BF)
    for c in acts:
        c.wait()


def finish(core, rows, back, back_in, own, own_in, act, act_in, vec, vec_in, weight):
    nodes, half = own.shape
    width = 2 * half
    return call(
        finish_kernel,
        (
            shape_of((nodes, width), BF),
            shape_of((nodes, width), BF),
            shape_of((8, width), F32),
        ),
        "finish",
        in_specs=[SMEM] + [VMEM] * 5 + [HBM] * 5,
        out_specs=(VMEM, VMEM, VMEM),
        scratch_shapes=[
            pltpu.VMEM(weight.shape, BF),
            pltpu.VMEM((2, nodes, half), BF),
            pltpu.VMEM((nodes, width), BF),
            pltpu.SemaphoreType.DMA((width // 512,)),
            pltpu.SemaphoreType.DMA((2,)),
            pltpu.SemaphoreType.DMA((2,)),
        ],
    )(scalars(core), rows, back, back_in, vec, vec_in, own, own_in, act, act_in, weight)


def on_device(
    size,
    features,
    weight,
    bias,
    gamma,
    beta,
    neighbours,
    edge_mask,
    node_mask,
    send_rows,
    send_mask,
    cotangent,
):
    nodes, width = features.shape
    sends = send_rows.shape[0]
    half = width // 2
    quarter = width // 4
    levels = size.bit_length() - 5

    me = lax.axis_index("dom")
    core = me & 1
    is0 = core == 0
    bits = {"f": (1, 2), "p": (2, 3), "q": (3, 1), "s": (2, 1), "z": (3, 3)}
    others = list(range(4, levels + 4))
    for b in others:
        bits[b] = (b, b)
    axes = ["f", "p", "q"] + others

    def bit_of(b):
        return (me >> b) & 1

    def bit(b):
        return jnp.where(is0, bit_of(bits[b][0]), bit_of(bits[b][1]))

    def weight_of(b):
        return jnp.where(is0, 1 << bits[b][0], 1 << bits[b][1])

    def peer(i, b):
        return i ^ (1 << bits[b][i & 1])

    first, sibling_first = bit("f"), jnp.where(is0, bit_of(2), bit_of(1))
    high, sibling_high = bit("p"), jnp.where(is0, bit_of(3), bit_of(2))

    def along(x, b):
        return lax.ppermute(x, "dom", [(i, peer(i, b)) for i in range(size)])

    def swap(x):
        return lax.ppermute(x, "dom", [(i, i ^ 1) for i in range(size)])

    token = [jnp.zeros((8, 128), F32)]

    def arrive(*x):
        *x, token[0] = lax.optimization_barrier((*x, token[0]))
        return x[0] if len(x) == 1 else x

    def tick():
        token[0] = tick_of(token[0])

    def start(generators):
        running = dict(generators)
        for k in running:
            next(running[k])
        done = {}

        def advance(k):
            try:
                next(running[k])
            except StopIteration as stop:
                done[k] = stop.value

        return advance, done

    live_row = jnp.where(send_mask > 0, send_rows, -1)[:, None]
    out_away, *out_keep = outgoing_rows(
        core, live_row, features, HALO_WIDTHS
    )
    outgoing = stack(out_keep, arrive(swap(out_away)))
    halo_rows = sends * size
    chip_rows = 2 * sends

    def gather_halo(x):
        for b in reversed(axes):
            received = along(x, b)
            yield
            x = stack_rows(x, arrive(received))
        return x

    generators = {k: gather_halo(x) for k, x in enumerate(outgoing)}
    advance, halo = start(generators)

    def hop():
        for k in generators:
            advance(k)

    live_neighbour = jnp.where(edge_mask > 0, neighbours, -1)
    packed = jnp.concatenate([live_neighbour, node_mask[:, None]], 1)
    place_of = jnp.arange(halo_rows)
    chip, row = place_of // chip_rows, place_of % chip_rows
    relative = 0
    for k, b in enumerate(axes):
        relative = relative + ((chip >> (len(axes) - 1 - k)) & 1) * weight_of(b)
    owner = (me ^ relative) ^ (row // sends)
    label = (nodes + owner * sends + row % sends)[None, :]
    packed, label = arrive(packed, label)
    sibling_packed = arrive(swap(packed))
    hop()
    features_in, cotangent_in = swap(features), swap(cotangent)
    constants = jnp.stack([bias, gamma, beta])
    packed = arrive(packed)
    own = arrive(*counts(packed, label))
    constants = arrive(constants)
    hop()
    features_in, cotangent_in, sibling_packed = arrive(features_in, cotangent_in, sibling_packed)
    sibling = arrive(*counts(sibling_packed, label))
    hop()
    for _ in range(levels):
        hop()

    agg_mine = aggregate(
        core, features, features_in, own, sibling, [halo[k] for k in generators]
    )
    agg_other = swap(agg_mine)
    mine_pair = along(agg_mine, "f")
    agg_other = arrive(agg_other)
    other_pair = along(agg_other, "f")
    z, stats = forward(
        core, agg_mine, agg_other, weight, constants, cotangent, cotangent_in, own[2], sibling[2]
    )

    same = (high == core).astype(jnp.int32)
    for k, b in enumerate(others + ["q", "p", "f"]):
        received = along(stats, b)
        if k == 0:
            mine_pair = arrive(mine_pair)
        if b == "f":
            other_pair = arrive(other_pair)
        stats = merge(stats, arrive(received), bit(b))
    nodes_args = (z, stats, constants, cotangent, cotangent_in, own[2], sibling[2])
    dz_send = dz_of(core, 1 - first, *nodes_args)

    dz_pair = along(dz_send, "f")
    aggs = (agg_mine, agg_other, mine_pair, other_pair)
    dz_send = arrive(dz_send)
    dz_keep = dz_of(core, first, *nodes_args)
    away = fetch(1 - same, *aggs)
    dz_keep, *away = arrive(dz_keep, *away)
    dz_pair = arrive(dz_pair)

    def weight_gradient(t):
        received = along(weight_part(*away, dz_keep, dz_pair, t), "p")
        yield
        part = weight_part(*keep, dz_keep, dz_pair, t)
        part = arrive(part)
        yield
        received = arrive(received)
        for b in axes[2:]:
            out, part = fold(part, received, bit(b))
            received = along(out, b)
            yield
            received = arrive(received)
        part = total_of(part, received)
        for b in others[::-1] + [LAST[0]]:
            received = along(part, b)
            yield
            part = join(part, arrive(received), bit(b))
        return part

    def reduce_halo():
        received, part = along(back_send, axes[0]), back_keep
        for b in axes[1:]:
            yield
            out, part = halve(part, arrive(received))
            received = along(out, b)
        yield
        return total_of(part, arrive(received))

    generators = {"d%d" % t: weight_gradient(t) for t in range(TILES)}
    advance, found = start(generators)
    groups = {k: [1, 1, len(others), len(others), 1] for k in generators}
    groups["h"] = [1, 1, 1, len(others)]
    tall = half // TILES
    tiles = range(TILES)
    shape = (width, width)
    if LAST[1] == "z":
        layers = bit_of(3), bit_of(3)
        steps = jnp.where(is0, half, tall // 2), jnp.where(is0, tall // 2, half)
        steps = steps, steps[::-1]
    else:
        layers = high, sibling_high
        steps = ((tall // 2, half),) * 2

    def pieces(own, sibling, away, other):
        placed = []
        for side, arrays in enumerate((own, sibling)):
            begin = core if side == 0 else 1 - core
            f = first if side == 0 else sibling_first
            inner, outer = steps[side]
            z = 1 - layers[side] if away else layers[side]
            for t, x in enumerate(arrays):
                row = t * tall + z * outer
                column = begin * half + (1 - f if other else f) * quarter
                placed.append((x, row, row + inner, column))
        return placed

    across, pair, here = [None] * TILES, [None] * TILES, [None] * TILES
    here_across, here_pair, pair_across = [None] * TILES, [None] * TILES, [None] * TILES
    for action in ORDER:
        if action == "K":
            keep = arrive(*fetch(same, *aggs))
            for k in generators:
                advance(k)
        elif action == "O":
            dz_scaled, act, act_away, vectors = arrive(*outputs(core, *nodes_args))
        elif action == "G":
            dz_scaled = arrive(dz_scaled)
            back_send, back_keep = arrive(
                *(back_part(core, own[0], sibling[0], dz_scaled, k, 2) for k in (1, 0))
            )
        elif action == "H":
            back_send = arrive(back_send)
            advance_halo, halo_part = start({"h": reduce_halo()})
        elif action == "B":
            dz_scaled = arrive(dz_scaled)
            kept_back, away_back = arrive(*own_back(core, own[1], sibling[1], dz_scaled))
            own_in, act_in, vectors_in = swap(away_back), swap(act_away), swap(vectors)
        elif action == "b":
            own_in, act_in, vectors_in = arrive(own_in, act_in, vectors_in)
        elif action == "t":
            tick()
        elif action in groups:
            step = advance_halo if action == "h" else advance
            for _ in range(groups[action].pop(0)):
                step(action)
            if action in found:
                t = list(generators).index(action)
                across[t], pair[t] = along(found[action], LAST[1]), along(found[action], "f")
                here[t] = swap(found[action])
        elif action == "e":
            here = [arrive(x) for x in here]
            part = [found[k] for k in generators]
            total = arrive(place(None, pieces(part, here, False, False), shape))
        elif action[0] == "x":
            t = int(action[1])
            across[t] = arrive(across[t])
            here_across[t], pair_across[t] = swap(across[t]), along(across[t], "f")
        elif action[0] == "p":
            t = int(action[1])
            pair[t] = arrive(pair[t])
            here_pair[t] = swap(pair[t])
        elif action == "R":
            back = halo_part["h"]
            back_in = arrive(swap(back[sends:]))
        elif action == "F":
            grad_features, activations, vectors = arrive(
                *finish(
                    core, live_row, back, back_in, kept_back, own_in, act, act_in, vectors, vectors_in, weight
                )
            )
        elif action == "P":
            here_across = [arrive(x) for x in here_across]
            here_pair = [arrive(x) for x in here_pair]
            total = place(
                total,
                pieces(across, here_across, True, False) + pieces(pair, here_pair, False, True),
                shape,
            )
            total = arrive(total)
    pair_across = [arrive(x) for x in pair_across]
    vectors = vectors + token[0][0, 0]
    here_pair_across = [swap(x) for x in pair_across]
    total = place(total, pieces(pair_across, here_pair_across, True, True), shape)
    return activations, grad_features, total, vectors[0], vectors[1], vectors[2]


def solution(mesh):
    size = mesh.shape["dom"]
    return jax.shard_map(
        functools.partial(on_device, size),
        mesh=mesh,
        in_specs=(
            P("dom", None),
            P(),
            P(),
            P(),
            P(),
            P("dom", None),
            P("dom", None),
            P("dom"),
            P("dom"),
            P("dom"),
            P("dom", None),
        ),
        out_specs=(P("dom", None), P("dom", None), P(), P(), P(), P()),
        check_vma=False,
    )
```
